32 devices in a mesh: groups: 2 (over y), sub: 4 (over z), rng: 2 (over x), chan: 2 (over core).
Axes of the slice: x: 2, y: 2, z: 4, core: 2. Of those that a mesh axis runs over, the one named last changes fastest.
Arguments:
- raw: bfloat16 [4, 2, 4096, 512], P('chan', None, ('groups', 'sub'), 'rng'), parts along dimension 2, may hold values from -6 to 6
- filt: float32 [4, 2, 16], P('chan'), may hold values from -1 to 1
- steer: bfloat16 [4, 256, 1024], P('sub'), may hold values from -0.1875 to 0.1875
- chan_w: float32 [4, 2], P('chan'), may hold values from -2 to 2
- merge_w: bfloat16 [4, 2, 2, 256, 256], P('sub'), may hold values from -1 to 1
- samp_index: int32 [8, 4, 8, 32], P(('sub', 'rng')), may hold values from 0 to 32767
- samp_weight: float32 [8, 4, 8, 32], P(('sub', 'rng')), may hold values from 0.1 to 1
- counts: int32 [8, 8], P(('sub', 'rng')), may hold values from 0 to 32, as said below
- pixel_id: int32 [8, 8, 32], P(('sub', 'rng')), may hold values from 0 to 4095
Outputs:
- cart: float32 [2, 65536], P(None, ('groups', 'sub', 'rng')), parts along dimension 1
The draws below stay inside these ranges and needn't reach their ends.
There are 2 independent parts, one for each index of `groups`. The reference program is written for one: setup_inputs(seed, part) draws one part's arguments, and reference() takes and returns one part's arrays. A program takes and returns all parts, laid end to end along the dimension named above; an argument that names none is the same for every part. Nothing has to cross between parts.
Inputs may be any that keep to these rules, and one draw needn't show every extreme that they name: `counts`: A block sends at most 32 live slots to one owner; some owners receive 32 from every block.
All inputs are finite; a program needn't handle non-finite values.
Results may differ from the reference program's by a relative error of at most 0.013.
Values may be sent and summed in bfloat16 or wider, within the bound.
No kernel may reach another device: no remote copies, remote signals or barrier semaphores. Data moves between devices by JAX's collectives and lax.ppermute only.
A program may use at most 64 MiB of HBM per device.

```python
import math
import jax
import jax.numpy as jnp
import numpy as np
from jax import lax

P_DEV = 512
R_DEV = 256
BEAMS = 128
KER = 16
CAP = 32
TAPS = 4
PIX_OWN = 4096
CHANNELS = 4
PULSES = 2048
RANGE = 512
LEVELS = 2
OWNERS = 8
N_SUB = 4
N_RNG = 2


def draw_merge_w(key, part):
    order_size = 2 * BEAMS
    shape = (N_SUB, LEVELS, 2, order_size, order_size)
    identity = jnp.eye(order_size, dtype=jnp.float32)
    diag_coef = jnp.array([0.6, 0.5], jnp.float32)[None, None, :, None, None]
    noise = jax.random.normal(jax.random.fold_in(key, 3), shape, jnp.float32)
    noise = noise * (0.4 / math.sqrt(order_size))
    return (diag_coef * identity + noise).astype(jnp.bfloat16)


def draw_counts(key, part):
    first_key, second_key = jax.random.split(jax.random.fold_in(key, 11))
    ranking = jax.random.permutation(first_key, OWNERS)
    busy = ranking < max(OWNERS // 4, 1)
    lighter = jax.random.randint(second_key, (OWNERS, OWNERS), 0, CAP // 2)
    return jnp.where(busy[None, :], CAP, lighter).astype(jnp.int32)


def set_ends(entries, key, low, largest):
    index_at = [jax.random.randint(jax.random.fold_in(key, axis), (), 0, length) for axis, length in enumerate(entries.shape)]
    widest = entries.shape.index(max(entries.shape))
    beside = index_at[:widest] + [(index_at[widest] + 1) % entries.shape[widest]] + index_at[widest + 1:]
    return entries.at[tuple(index_at)].set(low).at[tuple(beside)].set(largest)


def steps_of(own_key, shape, cuts, low, high):
    def one(axis_at, parts):
        draws = jax.random.uniform(jax.random.fold_in(jax.random.fold_in(own_key, 6), axis_at), (parts,), jnp.float32, low / len(cuts), high / len(cuts))
        return jnp.repeat(jnp.exp(draws), shape[axis_at] // parts).reshape((-1,) + (1,) * (len(shape) - axis_at - 1))

    gain = one(*cuts[0])
    for cut in cuts[1:]:
        gain = gain * one(*cut)
    return gain


def scatter_about(stream_key, shape, scale, most, shards=(), held_as=jnp.bfloat16):
    values = scale * jax.random.normal(stream_key, shape, jnp.float32)
    if shards:
        values = values * steps_of(stream_key, shape, shards, -0.22, 0.18)
    return jnp.clip(values, -most, most).astype(held_as)


def setup_inputs(seed: int = 0, part: int = 0) -> dict:
    seeds = jax.random.split(jax.random.key(seed), 10)
    part_splits = jax.random.split(jax.random.fold_in(seeds[9], part), 10)
    return {
        "raw": scatter_about(part_splits[0], (CHANNELS, 2, PULSES, RANGE), 1.0, 6.0, ((0, 2), (2, 4), (3, 2))),
        "filt": scatter_about(seeds[1], (CHANNELS, 2, KER), (2 * KER) ** -0.5, 1.0, ((0, 2),), jnp.float32),
        "steer": scatter_about(seeds[2], (N_SUB, 2 * BEAMS, 2 * P_DEV), (2 * P_DEV) ** -0.5, 0.1875, ((0, 4),)),
        "chan_w": scatter_about(seeds[3], (CHANNELS, 2), (2 * CHANNELS) ** -0.5, 2.0, ((0, 2),), jnp.float32),
        "merge_w": draw_merge_w(jax.random.fold_in(seeds[9], 71), part),
        "samp_index": set_ends(jax.random.randint(seeds[5], (OWNERS, TAPS, OWNERS, CAP), 0, BEAMS * R_DEV), jax.random.fold_in(seeds[5], 1), 0, (BEAMS * R_DEV) - 1).astype(jnp.int32),
        "samp_weight": jnp.clip(0.1 + 0.9 * jax.random.uniform(seeds[6], (OWNERS, TAPS, OWNERS, CAP), jnp.float32) ** steps_of(seeds[6], (OWNERS, TAPS, OWNERS, CAP), ((0, 8),), -0.2, 0.2), 0.1, 1.0),
        "counts": draw_counts(jax.random.fold_in(seeds[9], 71), part),
        "pixel_id": set_ends(jax.random.randint(seeds[8], (OWNERS, OWNERS, CAP), 0, PIX_OWN), jax.random.fold_in(seeds[8], 1), 0, PIX_OWN - 1).astype(jnp.int32),
    }


def compress_channel(operands):
    samples, taps = operands
    margin = KER // 2
    padded = jnp.pad(samples, ((0, 0), (0, 0), (margin, margin)))
    bin_count = samples.shape[2]
    acc_re = jnp.zeros((samples.shape[1], bin_count), jnp.float32)
    acc_im = jnp.zeros((samples.shape[1], bin_count), jnp.float32)
    for offset in range(KER):
        seg_re = padded[0, :, offset:offset + bin_count].astype(jnp.float32)
        seg_im = padded[1, :, offset:offset + bin_count].astype(jnp.float32)
        acc_re = acc_re + taps[0, offset] * seg_re - taps[1, offset] * seg_im
        acc_im = acc_im + taps[0, offset] * seg_im + taps[1, offset] * seg_re
    return jnp.stack([acc_re, acc_im], 0).astype(jnp.bfloat16)


def reference(raw, filt, steer, chan_w, merge_w, samp_index, samp_weight, counts, pixel_id):
    compressed = lax.map(compress_channel, (raw, filt))
    channel_count = raw.shape[0]
    bin_total = raw.shape[3]
    grouped = compressed.reshape(channel_count, 2, N_SUB, P_DEV, bin_total)
    grouped = grouped.transpose(2, 0, 1, 3, 4).reshape(N_SUB, channel_count, 2 * P_DEV, bin_total)

    def form_image(operands):
        block, matrix = operands
        images = jnp.einsum("ij,cjr->cir", matrix.astype(jnp.float32), block.astype(jnp.float32),
                            precision=lax.Precision.HIGHEST)
        img_re = images[:, :BEAMS]
        img_im = images[:, BEAMS:]
        weight_re = chan_w[:, 0][:, None, None]
        weight_im = chan_w[:, 1][:, None, None]
        summed_re = jnp.sum(weight_re * img_re - weight_im * img_im, axis=0)
        summed_im = jnp.sum(weight_re * img_im + weight_im * img_re, axis=0)
        return jnp.concatenate([summed_re, summed_im], 0).astype(jnp.bfloat16)

    polar = lax.map(form_image, (grouped, steer))
    for level_index in range(LEVELS):
        partner = np.arange(N_SUB) ^ (1 << level_index)
        other = polar[partner]
        mixed = jnp.einsum("sij,sjr->sir", merge_w[:, level_index, 0].astype(jnp.float32),
                           polar.astype(jnp.float32), precision=lax.Precision.HIGHEST)
        mixed = mixed + jnp.einsum("sij,sjr->sir", merge_w[:, level_index, 1].astype(jnp.float32),
                                   other.astype(jnp.float32), precision=lax.Precision.HIGHEST)
        polar = mixed.astype(jnp.bfloat16)
    blocks = polar.reshape(N_SUB, 2, BEAMS, N_RNG, R_DEV).transpose(0, 3, 1, 2, 4)
    blocks = blocks.reshape(OWNERS, 2, BEAMS * R_DEV)

    def contributions(block, index, weights, count):
        values = block.astype(jnp.float32)[:, index]
        summed = jnp.sum(values * weights[None], axis=1)
        live = (jnp.arange(CAP, dtype=jnp.int32)[None, :] < count[:, None]).astype(jnp.float32)
        return summed * live[None]

    every_part = jax.vmap(contributions)(blocks, samp_index, samp_weight, counts)
    flat_vals = every_part.transpose(1, 2, 0, 3)
    targets = pixel_id + (jnp.arange(OWNERS, dtype=jnp.int32) * PIX_OWN)[:, None, None]
    cart = jnp.zeros((2, OWNERS * PIX_OWN), jnp.float32)
    cart = cart.at[:, targets.reshape(-1)].add(flat_vals.reshape(2, -1))
    return cart
```

```python
import functools

import jax
import jax.numpy as jnp
from jax import lax
from jax.experimental import pallas as pl
from jax.experimental.pallas import tpu as pltpu
from jax.sharding import PartitionSpec as P

PIX_OWN = 4096
LANES = 128
ROW = 256
EDGE = 8
F32 = jnp.float32
BF16 = jnp.bfloat16
VMEM = pl.BlockSpec(memory_space=pltpu.VMEM)
SMEM = pl.BlockSpec(memory_space=pltpu.SMEM)
NT = (((1,), (1,)), ((), ()))


def dot(a, b):
    return jnp.dot(a, b, preferred_element_type=F32)


def dot_nt(a, b):
    return lax.dot_general(a, b, NT, preferred_element_type=F32)


def prepare_kernel(raw_ref, last_ref, index_ref, weight_ref, counts_ref, edge_ref, pack_ref):
    channels, _, _, bins = raw_ref.shape
    row = lax.broadcasted_iota(jnp.int32, (2 * EDGE, bins), 0)
    column = lax.broadcasted_iota(jnp.int32, (2 * EDGE, bins), 1)
    wanted = jnp.where(row < EDGE, row, row + bins - 2 * EDGE)
    pick = (column == wanted).astype(F32).astype(BF16)
    for c in range(channels):
        for part in range(2):
            edge_ref[c, part] = dot_nt(pick, raw_ref[c, part]).astype(BF16)
    size = last_ref.shape[3]
    pack_ref[:size, :] = last_ref[0, 0, 0]
    taps, owners, slots = index_ref.shape[1:]
    per_row = ROW // slots
    slot = lax.broadcasted_iota(jnp.int32, (taps, slots), 1)
    rows = []
    for first in range(0, owners, per_row):
        parts = []
        for o in range(first, first + per_row):
            index = index_ref[0, :, o, :]
            weight = jnp.where(slot < counts_ref[0, o], weight_ref[0, :, o, :], 0.0)
            coarse = weight.astype(BF16).astype(F32)
            parts.append(
                jnp.concatenate(
                    [
                        (index // bins).astype(F32),
                        (index % bins).astype(F32),
                        coarse,
                        weight - coarse,
                    ],
                    0,
                )
            )
        rows.append(jnp.concatenate(parts, 1))
    pack_ref[size:, :] = jnp.concatenate(rows, 0).astype(BF16)


def circulants(filt_ref, channel, part):
    row = lax.broadcasted_iota(jnp.int32, (LANES, LANES), 0)
    column = lax.broadcasted_iota(jnp.int32, (LANES, LANES), 1)
    place = (row - column + EDGE) & (LANES - 1)
    out = jnp.zeros((LANES, LANES), F32)
    for k in range(filt_ref.shape[2]):
        out = jnp.where(place == k, filt_ref[channel, part, k], out)
    return out


def band(filt_ref, channel, part, bins):
    ring = circulants(filt_ref, channel, part)
    row = lax.broadcasted_iota(jnp.int32, (LANES, LANES), 0)
    column = lax.broadcasted_iota(jnp.int32, (LANES, LANES), 1)
    far = column - row
    zero = jnp.zeros((LANES, LANES), BF16)
    near = jnp.where((far < 64) & (far > -64), ring, 0.0).astype(BF16)
    below = jnp.where(far >= 64, ring, 0.0).astype(BF16)
    above = jnp.where(far <= -64, ring, 0.0).astype(BF16)
    count = bins // LANES
    blocks = {0: near, 1: below, -1: above}
    return jnp.concatenate(
        [
            jnp.concatenate([blocks.get(i - o, zero) for o in range(count)], 1)
            for i in range(count)
        ],
        0,
    )


def turned(value, channel_ref, channel):
    half = value.shape[0] // 2
    re, im = value[:half], value[half:]
    wr, wi = channel_ref[channel, 0], channel_ref[channel, 1]
    return jnp.concatenate([wr * re - wi * im, wr * im + wi * re], 0)


def steered(steer_ref, x_re, x_im, product):
    pulses = steer_ref.shape[2] // 2
    s_re, s_im = steer_ref[0, :, :pulses], steer_ref[0, :, pulses:]
    direct = product(s_re, x_re) + product(s_im, x_im)
    cross = product(s_im, x_re) - product(s_re, x_im)
    return direct.astype(BF16), cross.astype(BF16)


def image_kernel(raw_ref, steer_ref, filt_ref, channel_ref, out_ref):
    channels, _, _, bins = raw_ref.shape
    total = jnp.zeros(out_ref.shape, F32)
    for c in range(channels):
        direct, cross = steered(steer_ref, raw_ref[c, 0], raw_ref[c, 1], dot)
        image = dot(direct, band(filt_ref, c, 0, bins)) + dot(cross, band(filt_ref, c, 1, bins))
        total = total + turned(image, channel_ref, c)
    out_ref[...] = total


def edge_kernel(main_ref, edge_ref, steer_ref, filt_ref, channel_ref, ends_ref, out_ref):
    channels = edge_ref.shape[0]
    bins = main_ref.shape[1]
    row = lax.broadcasted_iota(jnp.int32, (2 * EDGE, bins), 0)
    column = lax.broadcasted_iota(jnp.int32, (2 * EDGE, bins), 1)
    high = row < EDGE
    source = jnp.where(high, row + bins, row - 2 * EDGE)
    there = jnp.where(high, ends_ref[1], ends_ref[0]) > 0
    place = jnp.where(there, source - column + EDGE, -1)
    total = main_ref[...]
    for c in range(channels):
        direct, cross = steered(steer_ref, edge_ref[c, 0], edge_ref[c, 1], dot_nt)
        taps = []
        for part in range(2):
            out = jnp.zeros((2 * EDGE, bins), F32)
            for k in range(filt_ref.shape[2]):
                out = jnp.where(place == k, filt_ref[c, part, k], out)
            taps.append(out.astype(BF16))
        image = dot(direct, taps[0]) + dot(cross, taps[1])
        total = total + turned(image, channel_ref, c)
    out_ref[...] = total.astype(BF16)


def merge_kernel(weight_ref, own_ref, other_ref, out_ref):
    mixed = dot(weight_ref[0, 0, 0], own_ref[...]) + dot(weight_ref[0, 0, 1], other_ref[...])
    out_ref[...] = mixed.astype(BF16)


def sample_kernel(taps, slots, weight_ref, own_ref, other_ref, pack_ref, far_ref, out_ref):
    size, bins = own_ref.shape
    half = size // 2
    mixed = dot(weight_ref[0, 0, 0], own_ref[...]) + dot(weight_ref[0, 0, 1], other_ref[...])
    polar = mixed.astype(BF16)
    chunks = (pack_ref.shape[0] - size) // (4 * taps)
    per_row = ROW // slots
    owners = per_row * chunks
    bin_ids = lax.broadcasted_iota(jnp.int32, (bins, ROW), 0).astype(F32)
    beam_ids = lax.broadcasted_iota(jnp.int32, (half, ROW), 0).astype(F32)
    for block, (merge, ref) in enumerate(
        ((weight_ref[0, 1, 0], pack_ref), (far_ref[:size, :], far_ref))
    ):
        merged = dot(merge, polar).astype(BF16)
        for chunk in range(chunks):
            base = size + 4 * taps * chunk
            rows = ref[base : base + 4 * taps, :].astype(F32)
            sum_re = jnp.zeros((half, ROW), F32)
            sum_im = jnp.zeros((half, ROW), F32)
            for t in range(taps):
                beam = rows[t : t + 1]
                column = rows[taps + t : taps + t + 1]
                weight = rows[2 * taps + t : 2 * taps + t + 1] + rows[3 * taps + t : 3 * taps + t + 1]
                pick_bin = (bin_ids == column).astype(F32).astype(BF16)
                picked = dot(merged, pick_bin)
                pick_beam = jnp.where(beam_ids == beam, weight, 0.0)
                sum_re = sum_re + picked[:half] * pick_beam
                sum_im = sum_im + picked[half:] * pick_beam
            for part, value in enumerate((sum_re, sum_im)):
                flat = jnp.sum(value, axis=0, keepdims=True)
                lane = (2 * block + part) * slots
                for k in range(per_row):
                    o = chunk * per_row + k
                    piece = flat[:, k * slots : (k + 1) * slots]
                    out_ref[o : o + 1, lane : lane + slots] = piece
                    out_ref[owners + o : owners + o + 1, lane : lane + slots] = piece


def scatter_kernel(value_ref, pixel_ref, out_ref, flat_ref, place_ref):
    owners, slots = pixel_ref.shape[1:]
    total = value_ref[:owners, :] + value_ref[owners:, :]
    for b in range(owners):
        far = (b + owners // 2) % owners
        place_ref[0:1, b * slots : (b + 1) * slots] = pixel_ref[0, b : b + 1, :]
        for part in range(2):
            lane = part * slots
            flat_ref[part : part + 1, b * slots : (b + 1) * slots] = (
                total[b : b + 1, lane : lane + slots]
                + total[far : far + 1, 2 * slots + lane : 2 * slots + lane + slots]
            )
    count = owners * slots
    tall = PIX_OWN // LANES
    pixel = place_ref[...]
    high = lax.broadcasted_iota(jnp.int32, (tall, count), 0) == pixel // LANES
    low = lax.broadcasted_iota(jnp.int32, (LANES, count), 0) == pixel % LANES
    pick_low = low.astype(F32).astype(BF16)
    spread = jnp.concatenate(
        [jnp.where(high, flat_ref[part : part + 1, :], 0.0) for part in range(2)], 0
    )
    coarse = spread.astype(BF16)
    fine = (spread - coarse.astype(F32)).astype(BF16)
    image = dot_nt(coarse, pick_low) + dot_nt(fine, pick_low)
    for part in range(2):
        for h in range(tall):
            row = part * tall + h
            out_ref[part : part + 1, h * LANES : (h + 1) * LANES] = image[row : row + 1, :]


def shape(dims, dtype):
    return jax.ShapeDtypeStruct(dims, dtype)


def picked(array, *indices):
    dims = tuple(1 for _ in indices) + array.shape[len(indices) :]
    place = indices + (0,) * (array.ndim - len(indices))
    return pl.BlockSpec(dims, lambda i: place)


def call(kernel, out_shape, in_specs, out_specs, flops=0, nbytes=0, scratch=(), grid=None):
    extra = {} if grid is None else {"grid": grid}
    return pl.pallas_call(
        kernel,
        out_shape=out_shape,
        in_specs=in_specs,
        out_specs=out_specs,
        scratch_shapes=list(scratch),
        cost_estimate=pl.CostEstimate(flops=flops, bytes_accessed=nbytes, transcendentals=0),
        compiler_params=pltpu.CompilerParams(vmem_limit_bytes=48 * 2**20),
        **extra,
    )


def whole(array):
    return pl.BlockSpec(array.shape, lambda i: (0,) * array.ndim)


def swapped(value, axis, bit):
    return lax.ppermute(value, axis, [(i, i ^ 1 << bit) for i in range(lax.axis_size(axis))])


def neighbour_edges(edges):
    count = lax.axis_size("rng")
    if count == 2:
        return lax.ppermute(edges, "rng", [(0, 1), (1, 0)])
    after = lax.ppermute(edges, "rng", [(i + 1, i) for i in range(count - 1)])
    before = lax.ppermute(edges, "rng", [(i, i + 1) for i in range(count - 1)])
    return jnp.concatenate([after[:, :, :EDGE], before[:, :, EDGE:]], 2)


def local(raw, filt, steer, chan_w, merge_w, samp_index, samp_weight, counts, pixel_id):
    channels, _, pulses, bins = raw.shape
    size = steer.shape[1]
    levels = merge_w.shape[1]
    taps, owners, slots = samp_index.shape[1:]
    extra = 4 * taps * owners * slots // ROW
    edge_dims = (channels, 2, 2 * EDGE, pulses)
    edges, pack = call(
        prepare_kernel,
        (shape(edge_dims, BF16), shape((size + extra, ROW), BF16)),
        [
            whole(raw),
            pl.BlockSpec((1, 1, 1, size, size), lambda i: (0, levels - 1, 1, 0, 0)),
            whole(samp_index),
            whole(samp_weight),
            SMEM,
        ],
        (pl.BlockSpec(edge_dims, lambda i: (0, 0, 0, 0)), pl.BlockSpec((size + extra, ROW), lambda i: (0, 0))),
        flops=2**26,
        nbytes=2**20,
        grid=(1,),
    )(raw, merge_w, samp_index, samp_weight, counts)
    beside = neighbour_edges(edges)
    far = swapped(pack, "sub", levels - 1)
    main = call(
        image_kernel,
        shape((size, bins), F32),
        [VMEM, VMEM, SMEM, SMEM],
        VMEM,
        flops=2**30,
        nbytes=2**21,
    )(raw, steer, filt, chan_w)
    place = lax.axis_index("rng")
    ends = jnp.stack([place > 0, place < lax.axis_size("rng") - 1]).astype(jnp.int32)
    polar = call(
        edge_kernel,
        shape((size, bins), BF16),
        [VMEM, VMEM, VMEM, SMEM, SMEM, SMEM],
        VMEM,
        flops=2**27,
        nbytes=2**20,
    )(main, beside, steer, filt, chan_w, ends)
    for level in range(levels - 2):
        other = swapped(polar, "sub", level)
        polar = call(
            merge_kernel,
            shape((size, bins), BF16),
            [
                pl.BlockSpec((1, 1, 2, size, size), lambda i, level=level: (0, level, 0, 0, 0)),
                whole(polar),
                whole(other),
            ],
            pl.BlockSpec((size, bins), lambda i: (0, 0)),
            grid=(1,),
        )(merge_w, polar, other)
    other = swapped(polar, "sub", levels - 2)
    outgoing = call(
        functools.partial(sample_kernel, taps, slots),
        shape((2 * owners, 4 * slots), F32),
        [
            VMEM,
            VMEM,
            VMEM,
            VMEM,
            VMEM,
        ],
        VMEM,
        flops=2**28,
        nbytes=2**20,
    )(merge_w[:, levels - 2 :], polar, other, pack, far)
    arrived = lax.all_to_all(
        outgoing, ("chan", "sub", "rng"), split_axis=0, concat_axis=0, tiled=True
    )
    return call(
        scatter_kernel,
        shape((2, PIX_OWN), F32),
        [VMEM, VMEM],
        VMEM,
        scratch=[
            pltpu.VMEM((2, owners * slots), F32),
            pltpu.VMEM((1, owners * slots), jnp.int32),
        ],
    )(arrived, pixel_id)


def solution(mesh):
    placed = (
        P("chan", None, ("groups", "sub"), "rng"),
        P("chan", None, None),
        P("sub", None, None),
        P("chan", None),
        P("sub", None, None, None, None),
        P(("sub", "rng"), None, None, None),
        P(("sub", "rng"), None, None, None),
        P(("sub", "rng"), None),
        P(("sub", "rng"), None, None),
    )
    return jax.shard_map(
        local,
        mesh=mesh,
        in_specs=placed,
        out_specs=P(None, ("groups", "sub", "rng")),
        check_vma=False,
    )
```

```python
import functools

import jax
import jax.numpy as jnp
from jax import lax
from jax.experimental import pallas as pl
from jax.experimental.pallas import tpu as pltpu
from jax.sharding import PartitionSpec as P

PIX_OWN = 4096
LANES = 128
ROW = 256
EDGE = 8
F32 = jnp.float32
BF16 = jnp.bfloat16
VMEM = pl.BlockSpec(memory_space=pltpu.VMEM)
SMEM = pl.BlockSpec(memory_space=pltpu.SMEM)
NT = (((1,), (1,)), ((), ()))


def dot(a, b):
    return jnp.dot(a, b, preferred_element_type=F32)


def dot_nt(a, b):
    return lax.dot_general(a, b, NT, preferred_element_type=F32)


def rim_kernel(raw_ref, edge_ref):
    channels, _, _, bins = raw_ref.shape
    row = lax.broadcasted_iota(jnp.int32, (2 * EDGE, bins), 0)
    column = lax.broadcasted_iota(jnp.int32, (2 * EDGE, bins), 1)
    wanted = jnp.where(row < EDGE, row, row + bins - 2 * EDGE)
    pick = (column == wanted).astype(F32).astype(BF16)
    for c in range(channels):
        for part in range(2):
            edge_ref[c, part] = dot_nt(pick, raw_ref[c, part]).astype(BF16)


def prepare_kernel(
    bins, chan_axis, merge_ref, index_ref, weight_ref, filt_ref, chan_ref, counts_ref,
    pack_ref, band_ref, end_ref, mix_ref,
):
    channels = filt_ref.shape[0]
    half = merge_ref.shape[3] // 2
    last = merge_ref.shape[1] - 1
    core = lax.axis_index(chan_axis) % 2
    rows = pl.ds(pl.multiple_of(core * half, half), half)
    pack_ref[:half, :] = merge_ref[0, last, 1, rows, :]
    taps = filt_ref.shape[2]
    row = lax.broadcasted_iota(jnp.int32, (LANES, LANES), 0)
    column = lax.broadcasted_iota(jnp.int32, (LANES, LANES), 1)
    far = column - row
    place = (EDGE - far) & (LANES - 1)
    rings = [[jnp.zeros((LANES, LANES), F32) for _ in range(2)] for _ in range(channels)]
    for k in range(taps):
        here = place == k
        for c in range(channels):
            for part in range(2):
                rings[c][part] = jnp.where(here, filt_ref[c, part, k], rings[c][part])
    zero = jnp.zeros((LANES, LANES), BF16)
    count = bins // LANES
    for c in range(channels):
        for part in range(2):
            ring = rings[c][part]
            blocks = {
                0: jnp.where((far < 64) & (far > -64), ring, 0.0).astype(BF16),
                1: jnp.where(far >= 64, ring, 0.0).astype(BF16),
                -1: jnp.where(far <= -64, ring, 0.0).astype(BF16),
            }
            for i in range(count):
                for o in range(count):
                    band_ref[
                        c, part, i * LANES : (i + 1) * LANES, o * LANES : (o + 1) * LANES
                    ] = blocks.get(i - o, zero)
    row = lax.broadcasted_iota(jnp.int32, (2 * EDGE, bins), 0)
    column = lax.broadcasted_iota(jnp.int32, (2 * EDGE, bins), 1)
    place = jnp.where(row < EDGE, row + bins, row - 2 * EDGE) - column + EDGE
    tails = [[jnp.zeros((2 * EDGE, bins), F32) for _ in range(2)] for _ in range(channels)]
    for k in range(taps):
        here = place == k
        for c in range(channels):
            for part in range(2):
                tails[c][part] = jnp.where(here, filt_ref[c, part, k], tails[c][part])
    nothing = jnp.zeros((2 * EDGE, bins), BF16)
    for c in range(channels):
        re, im = tails[c]
        for d in range(channels):
            quads = [re, -im, im, re]
            for q in range(4):
                top = (q // 2) * 2 * channels + 2 * d + q % 2
                end_ref[
                    top * 2 * EDGE : (top + 1) * 2 * EDGE, c * bins : (c + 1) * bins
                ] = quads[q].astype(BF16) if c == d else nothing
        for part in range(2):
            mix_ref[8 * (2 * c + part) : 8 * (2 * c + part + 1), :] = jnp.full(
                (8, bins), chan_ref[c, part], F32
            )
    taps, owners, slots = index_ref.shape[1:]
    per_row = ROW // slots
    slot = lax.broadcasted_iota(jnp.int32, (taps, slots), 1)
    lines = []
    for first in range(0, owners, per_row):
        parts = []
        for o in range(first, first + per_row):
            index = index_ref[0, :, o, :]
            weight = jnp.where(slot < counts_ref[0, o], weight_ref[0, :, o, :], 0.0)
            coarse = weight.astype(BF16).astype(F32)
            parts.append(
                jnp.concatenate(
                    [
                        (index // bins).astype(F32),
                        (index % bins).astype(F32),
                        coarse,
                        weight - coarse,
                    ],
                    0,
                )
            )
        lines.append(jnp.concatenate(parts, 1))
    pack_ref[half:, :] = jnp.concatenate(lines, 0).astype(BF16)


def turned(value, mix_ref, channel):
    half = value.shape[0] // 2
    re, im = value[:half], value[half:]
    wr = mix_ref[16 * channel : 16 * channel + 1, :]
    wi = mix_ref[16 * channel + 8 : 16 * channel + 9, :]
    return jnp.concatenate([wr * re - wi * im, wr * im + wi * re], 0)


def image_kernel(raw_ref, steer_ref, band_ref, mix_ref, out_ref):
    channels, _, pulses, _ = raw_ref.shape
    s_re, s_im = steer_ref[0, :, :pulses], steer_ref[0, :, pulses:]
    total = jnp.zeros(out_ref.shape, F32)
    for c in range(channels):
        x_re, x_im = raw_ref[c, 0], raw_ref[c, 1]
        direct = (dot(s_re, x_re) + dot(s_im, x_im)).astype(BF16)
        cross = (dot(s_im, x_re) - dot(s_re, x_im)).astype(BF16)
        image = dot(direct, band_ref[c, 0]) + dot(cross, band_ref[c, 1])
        total = total + turned(image, mix_ref, c)
    out_ref[...] = total


def edge_kernel(rng_axis, rng_size, main_ref, edge_ref, steer_ref, end_ref, mix_ref, out_ref):
    channels, _, _, pulses = edge_ref.shape
    bins = main_ref.shape[1]
    count = channels * 4 * EDGE
    block = lax.axis_index(rng_axis)
    row = lax.broadcasted_iota(jnp.int32, (count, pulses), 0)
    below = (row & EDGE) > 0
    first = jnp.where(block > 0, 1.0, 0.0)
    last = jnp.where(block < rng_size - 1, 1.0, 0.0)
    keep = jnp.where(below, first, last).astype(BF16)
    edges = edge_ref[...].reshape(count, pulses) * keep
    nothing = jnp.zeros((count, pulses), BF16)
    taken = dot_nt(steer_ref[0, :, :pulses], jnp.concatenate([edges, nothing], 0))
    taken = taken + dot_nt(steer_ref[0, :, pulses:], jnp.concatenate([nothing, edges], 0))
    images = dot(taken.astype(BF16), end_ref[...])
    total = main_ref[...]
    for c in range(channels):
        total = total + turned(images[:, c * bins : (c + 1) * bins], mix_ref, c)
    out_ref[...] = total.astype(BF16)


def merge_kernel(weight_ref, own_ref, other_ref, out_ref):
    mixed = dot(weight_ref[0, 0, 0], own_ref[...]) + dot(weight_ref[0, 0, 1], other_ref[...])
    out_ref[...] = mixed.astype(BF16)


def sample_kernel(
    taps, slots, chan_axis, weight_ref, own_ref, other_ref, pack_ref, near_ref, far_ref, out_ref
):
    size, bins = own_ref.shape
    half = size // 2
    mixed = dot(weight_ref[0, 0, 0], own_ref[...]) + dot(weight_ref[0, 0, 1], other_ref[...])
    polar = mixed.astype(BF16)
    chunks = (pack_ref.shape[0] - half) // (4 * taps)
    per_row = ROW // slots
    owners = per_row * chunks
    even = lax.axis_index(chan_axis) % 2 == 0
    bin_ids = lax.broadcasted_iota(jnp.int32, (bins, ROW), 0).astype(F32)
    beam_ids = lax.broadcasted_iota(jnp.int32, (half, ROW), 0).astype(F32)
    for block, (merges, ref) in enumerate(
        (
            ((weight_ref[0, 1, 0, :half], weight_ref[0, 1, 0, half:]), pack_ref),
            ((near_ref[:half, :], far_ref[:half, :]), near_ref),
        )
    ):
        merged = [dot(merge, polar).astype(BF16) for merge in merges]
        for chunk in range(chunks):
            base = half + 4 * taps * chunk
            rows = ref[base : base + 4 * taps, :].astype(F32)
            sums = [jnp.zeros((half, ROW), F32) for _ in range(2)]
            for t in range(taps):
                beam = rows[t : t + 1]
                column = rows[taps + t : taps + t + 1]
                weight = rows[2 * taps + t : 2 * taps + t + 1] + rows[3 * taps + t : 3 * taps + t + 1]
                pick_bin = (bin_ids == column).astype(F32).astype(BF16)
                pick_beam = jnp.where(beam_ids == beam, weight, 0.0)
                for part in range(2):
                    sums[part] = sums[part] + dot(merged[part], pick_bin) * pick_beam
            flat = [jnp.sum(value, axis=0, keepdims=True) for value in sums]
            if block == 1:
                flat = [jnp.where(even, flat[0], flat[1]), jnp.where(even, flat[1], flat[0])]
            for part in range(2):
                lane = (2 * block + part) * slots
                for k in range(per_row):
                    o = chunk * per_row + k
                    piece = flat[part][:, k * slots : (k + 1) * slots]
                    out_ref[o : o + 1, lane : lane + slots] = piece
                    out_ref[owners + o : owners + o + 1, lane : lane + slots] = piece


def scatter_kernel(value_ref, pixel_ref, out_ref, flat_ref, place_ref):
    owners, slots = pixel_ref.shape[1:]
    total = value_ref[:owners, :] + value_ref[owners:, :]
    for b in range(owners):
        far = (b + owners // 2) % owners
        place_ref[0:1, b * slots : (b + 1) * slots] = pixel_ref[0, b : b + 1, :]
        for part in range(2):
            lane = part * slots
            flat_ref[part : part + 1, b * slots : (b + 1) * slots] = (
                total[b : b + 1, lane : lane + slots]
                + total[far : far + 1, 2 * slots + lane : 2 * slots + lane + slots]
            )
    count = owners * slots
    tall = PIX_OWN // LANES
    pixel = place_ref[...]
    high = lax.broadcasted_iota(jnp.int32, (tall, count), 0) == pixel // LANES
    low = lax.broadcasted_iota(jnp.int32, (LANES, count), 0) == pixel % LANES
    pick_low = low.astype(F32).astype(BF16)
    spread = jnp.concatenate(
        [jnp.where(high, flat_ref[part : part + 1, :], 0.0) for part in range(2)], 0
    )
    coarse = spread.astype(BF16)
    fine = (spread - coarse.astype(F32)).astype(BF16)
    image = dot_nt(coarse, pick_low) + dot_nt(fine, pick_low)
    for part in range(2):
        for h in range(tall):
            row = part * tall + h
            out_ref[part : part + 1, h * LANES : (h + 1) * LANES] = image[row : row + 1, :]


def shape(dims, dtype):
    return jax.ShapeDtypeStruct(dims, dtype)


def call(kernel, out_shape, in_specs, out_specs, flops=0, nbytes=0, scratch=(), grid=None):
    extra = {} if grid is None else {"grid": grid}
    return pl.pallas_call(
        kernel,
        out_shape=out_shape,
        in_specs=in_specs,
        out_specs=out_specs,
        scratch_shapes=list(scratch),
        cost_estimate=pl.CostEstimate(flops=flops, bytes_accessed=nbytes, transcendentals=0),
        compiler_params=pltpu.CompilerParams(vmem_limit_bytes=24 * 2**20),
        **extra,
    )


def whole(array):
    return pl.BlockSpec(array.shape, lambda i: (0,) * array.ndim)


def swapped(value, axis, bit):
    return lax.ppermute(value, axis, [(i, i ^ 1 << bit) for i in range(lax.axis_size(axis))])


def neighbour_edges(edges):
    count = lax.axis_size("rng")
    if count == 2:
        return lax.ppermute(edges, "rng", [(0, 1), (1, 0)])
    after = lax.ppermute(edges, "rng", [(i + 1, i) for i in range(count - 1)])
    before = lax.ppermute(edges, "rng", [(i, i + 1) for i in range(count - 1)])
    return jnp.concatenate([after[:, :, :EDGE], before[:, :, EDGE:]], 2)


def local(raw, filt, steer, chan_w, merge_w, samp_index, samp_weight, counts, pixel_id):
    channels, _, pulses, bins = raw.shape
    size = steer.shape[1]
    levels = merge_w.shape[1]
    taps, owners, slots = samp_index.shape[1:]
    extra = 4 * taps * owners * slots // ROW
    edges = call(
        rim_kernel,
        shape((channels, 2, 2 * EDGE, pulses), BF16),
        [VMEM],
        VMEM,
        flops=2**32,
        nbytes=2**24,
    )(raw)
    beside = neighbour_edges(edges)
    pack, bands, ends, mix = call(
        functools.partial(prepare_kernel, bins, "chan"),
        (
            shape((size // 2 + extra, ROW), BF16),
            shape((channels, 2, bins, bins), BF16),
            shape((channels * 8 * EDGE, channels * bins), BF16),
            shape((16 * channels, bins), F32),
        ),
        [VMEM] * 3 + [SMEM] * 3,
        (VMEM,) * 4,
        flops=2**28,
        nbytes=2**20,
    )(merge_w, samp_index, samp_weight, filt, chan_w, counts)
    near = swapped(pack, "sub", levels - 1)
    main = call(
        image_kernel,
        shape((size, bins), F32),
        [VMEM] * 4,
        VMEM,
        flops=2**30,
        nbytes=2**21,
    )(raw, steer, bands, mix)
    polar = call(
        functools.partial(edge_kernel, "rng", lax.axis_size("rng")),
        shape((size, bins), BF16),
        [VMEM] * 5,
        VMEM,
        flops=2**27,
        nbytes=2**20,
    )(main, beside, steer, ends, mix)
    far = swapped(lax.optimization_barrier((polar, near))[1], "chan", 0)
    for level in range(levels - 2):
        other = swapped(polar, "sub", level)
        polar = call(
            merge_kernel,
            shape((size, bins), BF16),
            [
                pl.BlockSpec((1, 1, 2, size, size), lambda i, level=level: (0, level, 0, 0, 0)),
                whole(polar),
                whole(other),
            ],
            pl.BlockSpec((size, bins), lambda i: (0, 0)),
            grid=(1,),
        )(merge_w, polar, other)
    other = swapped(polar, "sub", levels - 2)
    outgoing = call(
        functools.partial(sample_kernel, taps, slots, "chan"),
        shape((2 * owners, 4 * slots), F32),
        [VMEM] * 6,
        VMEM,
        flops=2**28,
        nbytes=2**20,
    )(merge_w[:, levels - 2 :], polar, other, pack, near, far)
    values = lax.all_to_all(
        outgoing, ("chan", "sub", "rng"), split_axis=0, concat_axis=0, tiled=True
    )
    return call(
        scatter_kernel,
        shape((2, PIX_OWN), F32),
        [VMEM, VMEM],
        VMEM,
        scratch=[
            pltpu.VMEM((2, owners * slots), F32),
            pltpu.VMEM((1, owners * slots), jnp.int32),
        ],
    )(values, pixel_id)


def solution(mesh):
    placed = (
        P("chan", None, ("groups", "sub"), "rng"),
        P("chan", None, None),
        P("sub", None, None),
        P("chan", None),
        P("sub", None, None, None, None),
        P(("sub", "rng"), None, None, None),
        P(("sub", "rng"), None, None, None),
        P(("sub", "rng"), None),
        P(("sub", "rng"), None, None),
    )
    return jax.shard_map(
        local,
        mesh=mesh,
        in_specs=placed,
        out_specs=P(None, ("groups", "sub", "rng")),
        check_vma=False,
    )
```

```python
import functools

import jax
import jax.numpy as jnp
from jax import lax
from jax.experimental import pallas as pl
from jax.experimental.pallas import tpu as pltpu
from jax.sharding import PartitionSpec as P

PIX_OWN = 4096
LANES = 128
ROW = 256
EDGE = 8
F32 = jnp.float32
BF16 = jnp.bfloat16
VMEM = pl.BlockSpec(memory_space=pltpu.VMEM)
NT = (((1,), (1,)), ((), ()))


def dot(a, b):
    return jnp.dot(a, b, preferred_element_type=F32)


def dot_nt(a, b):
    return lax.dot_general(a, b, NT, preferred_element_type=F32)


def own_rims(rng_axis, rng_size, bins):
    if rng_size == 2:
        return [jnp.where(lax.axis_index(rng_axis) == 0, bins - EDGE, 0)]
    return [0, bins - EDGE]


def far_rims(rng_axis, rng_size, bins):
    if rng_size == 2:
        return [jnp.where(lax.axis_index(rng_axis) == 0, bins, -EDGE)]
    return [bins, -EDGE]


def rim_kernel(rng_axis, rng_size, raw_ref, edge_ref):
    channels, _, _, bins = raw_ref.shape
    count = channels * 2 * EDGE
    row = lax.broadcasted_iota(jnp.int32, (2 * EDGE, LANES), 0)
    column = lax.broadcasted_iota(jnp.int32, (2 * EDGE, LANES), 1)
    for side, first in enumerate(own_rims(rng_axis, rng_size, bins)):
        lane = pl.multiple_of(first - first % LANES, LANES)
        pick = (column == (row & (EDGE - 1)) + first - lane).astype(F32).astype(BF16)
        lines = [
            dot_nt(pick, raw_ref[c, part, :, pl.ds(lane, LANES)])[:EDGE]
            for c in range(channels)
            for part in range(2)
        ]
        edge_ref[side * count : (side + 1) * count, :] = jnp.concatenate(lines, 0).astype(BF16)


def pack_kernel(shift, chan_axis, merge_ref, index_ref, weight_ref, counts_ref, pack_ref):
    half = merge_ref.shape[3] // 2
    last = merge_ref.shape[1] - 1
    core = lax.axis_index(chan_axis) % 2
    rows = pl.ds(pl.multiple_of(core * half, half), half)
    pack_ref[:half, :] = merge_ref[0, last, 1, rows, :]
    taps, owners, slots = index_ref.shape[1:]
    per_row = ROW // slots
    slot = lax.broadcasted_iota(jnp.int32, (taps, slots), 1)
    for first in range(0, owners, per_row):
        index = jnp.concatenate([index_ref[0, :, first + k, :] for k in range(per_row)], 1)
        weight = jnp.concatenate(
            [
                jnp.where(slot < counts_ref[:, first + k : first + k + 1], weight_ref[0, :, first + k, :], 0.0)
                for k in range(per_row)
            ],
            1,
        )
        coarse = weight.astype(BF16).astype(F32)
        beam = (index >> shift).astype(F32)
        column = (index & ((1 << shift) - 1)).astype(F32)
        lines = jnp.concatenate([beam, column, coarse, weight - coarse], 0).astype(BF16)
        base = half + 4 * taps * (first // per_row)
        pack_ref[base : base + 4 * taps, :] = lines


def filter_kernel(bins, rng_axis, rng_size, filt_ref, chan_ref, band_ref, end_ref, mix_ref):
    channels, parts, taps = filt_ref.shape
    rows = jnp.concatenate([filt_ref[c] for c in range(channels)], 0).astype(BF16)
    source = lax.broadcasted_iota(jnp.int32, (taps, LANES), 0)
    target = lax.broadcasted_iota(jnp.int32, (taps, LANES), 1)
    mirror = (source == ((EDGE - target) & (LANES - 1))).astype(F32).astype(BF16)
    bases = dot(rows, mirror)
    row = lax.broadcasted_iota(jnp.int32, (LANES, LANES), 0)
    column = lax.broadcasted_iota(jnp.int32, (LANES, LANES), 1)
    far = column - row
    zero = jnp.zeros((LANES, LANES), BF16)
    count = bins // LANES
    firsts = far_rims(rng_axis, rng_size, bins)
    tails = []
    for c in range(channels):
        tails.append([])
        for part in range(parts):
            base = bases[c * parts + part : c * parts + part + 1]
            ring = pltpu.roll(
                jnp.broadcast_to(base, (LANES, LANES)), 0, 1, stride=1, stride_axis=0
            )
            below = jnp.where(far >= 64, ring, 0.0)
            above = jnp.where(far <= -64, ring, 0.0)
            blocks = {
                0: jnp.where((far < 64) & (far > -64), ring, 0.0).astype(BF16),
                1: below.astype(BF16),
                -1: above.astype(BF16),
            }
            for i in range(count):
                for o in range(count):
                    band_ref[
                        c, part, i * LANES : (i + 1) * LANES, o * LANES : (o + 1) * LANES
                    ] = blocks.get(i - o, zero)
            blank = jnp.zeros((EDGE, bins - LANES), F32)
            ahead = jnp.concatenate([blank, below[:EDGE]], 1)
            behind = jnp.concatenate([above[LANES - EDGE :], blank], 1)
            if rng_size == 2:
                tails[c].append([jnp.where(firsts[0] > 0, ahead, behind)])
            else:
                tails[c].append([ahead, behind])
    nothing = jnp.zeros((2 * EDGE, bins), BF16)
    for side in range(len(firsts)):
        for c in range(channels):
            re, im = tails[c][0][side], tails[c][1][side]
            blocks = [jnp.concatenate(pair, 0).astype(BF16) for pair in ((re, -im), (im, re))]
            for d in range(channels):
                for q in range(2):
                    top = ((q * len(firsts) + side) * channels + d) * 2 * EDGE
                    end_ref[top : top + 2 * EDGE, c * bins : (c + 1) * bins] = (
                        blocks[q] if c == d else nothing
                    )
    for c in range(channels):
        for part in range(parts):
            mix_ref[8 * (2 * c + part) : 8 * (2 * c + part + 1), :] = jnp.broadcast_to(
                chan_ref[c : c + 1, part : part + 1], (8, bins)
            )


def turned(value, mix_ref, channel):
    half = value.shape[0] // 2
    re, im = value[:half], value[half:]
    wr = mix_ref[16 * channel : 16 * channel + 1, :]
    wi = mix_ref[16 * channel + 8 : 16 * channel + 9, :]
    return jnp.concatenate([wr * re - wi * im, wr * im + wi * re], 0)


def image_kernel(raw_ref, steer_ref, band_ref, mix_ref, out_ref):
    channels, _, pulses, _ = raw_ref.shape
    s_re, s_im = steer_ref[0, :, :pulses], steer_ref[0, :, pulses:]
    total = jnp.zeros(out_ref.shape, F32)
    for c in range(channels):
        x_re, x_im = raw_ref[c, 0], raw_ref[c, 1]
        direct = (dot(s_re, x_re) + dot(s_im, x_im)).astype(BF16)
        cross = (dot(s_im, x_re) - dot(s_re, x_im)).astype(BF16)
        image = dot(direct, band_ref[c, 0]) + dot(cross, band_ref[c, 1])
        total = total + turned(image, mix_ref, c)
    out_ref[...] = total


def edge_kernel(main_ref, edge_ref, steer_ref, end_ref, mix_ref, out_ref):
    count, pulses = edge_ref.shape
    bins = main_ref.shape[1]
    edges = edge_ref[...]
    nothing = jnp.zeros((count, pulses), BF16)
    taken = dot_nt(steer_ref[0, :, :pulses], jnp.concatenate([edges, nothing], 0))
    taken = taken + dot_nt(steer_ref[0, :, pulses:], jnp.concatenate([nothing, edges], 0))
    images = dot(taken.astype(BF16), end_ref[...])
    total = main_ref[...]
    for c in range(end_ref.shape[1] // bins):
        total = total + turned(images[:, c * bins : (c + 1) * bins], mix_ref, c)
    out_ref[...] = total.astype(BF16)


def merge_kernel(weight_ref, own_ref, other_ref, out_ref):
    mixed = dot(weight_ref[0, 0, 0], own_ref[...]) + dot(weight_ref[0, 0, 1], other_ref[...])
    out_ref[...] = mixed.astype(BF16)


def sample_kernel(
    taps, slots, chan_axis, weight_ref, own_ref, other_ref, pack_ref, near_ref, far_ref, out_ref
):
    size, bins = own_ref.shape
    half = size // 2
    mixed = dot(weight_ref[0, 0, 0], own_ref[...]) + dot(weight_ref[0, 0, 1], other_ref[...])
    polar = mixed.astype(BF16)
    chunks = (pack_ref.shape[0] - half) // (4 * taps)
    per_row = ROW // slots
    owners = per_row * chunks
    even = lax.axis_index(chan_axis) % 2 == 0
    bin_ids = lax.broadcasted_iota(jnp.int32, (bins, ROW), 0).astype(F32)
    beam_ids = lax.broadcasted_iota(jnp.int32, (half, ROW), 0).astype(F32)
    for block, (merges, ref) in enumerate(
        (
            ((weight_ref[0, 1, 0, :half], weight_ref[0, 1, 0, half:]), pack_ref),
            ((near_ref[:half, :], far_ref[:half, :]), near_ref),
        )
    ):
        merged = [dot(merge, polar).astype(BF16) for merge in merges]
        for chunk in range(chunks):
            base = half + 4 * taps * chunk
            rows = ref[base : base + 4 * taps, :].astype(F32)
            sums = [jnp.zeros((half, ROW), F32) for _ in range(2)]
            for t in range(taps):
                beam = rows[t : t + 1]
                column = rows[taps + t : taps + t + 1]
                weight = rows[2 * taps + t : 2 * taps + t + 1] + rows[3 * taps + t : 3 * taps + t + 1]
                pick_bin = (bin_ids == column).astype(F32).astype(BF16)
                pick_beam = jnp.where(beam_ids == beam, weight, 0.0)
                for part in range(2):
                    sums[part] = sums[part] + dot(merged[part], pick_bin) * pick_beam
            flat = [jnp.sum(value, axis=0, keepdims=True) for value in sums]
            if block == 1:
                flat = [jnp.where(even, flat[0], flat[1]), jnp.where(even, flat[1], flat[0])]
            for part in range(2):
                lane = (2 * block + part) * slots
                for k in range(per_row):
                    o = chunk * per_row + k
                    piece = flat[part][:, k * slots : (k + 1) * slots]
                    out_ref[o : o + 1, lane : lane + slots] = piece
                    out_ref[owners + o : owners + o + 1, lane : lane + slots] = piece


def scatter_kernel(value_ref, pixel_ref, out_ref, flat_ref, place_ref):
    owners, slots = pixel_ref.shape[1:]
    total = value_ref[:owners, :] + value_ref[owners:, :]
    for b in range(owners):
        far = (b + owners // 2) % owners
        place_ref[0:1, b * slots : (b + 1) * slots] = pixel_ref[0, b : b + 1, :]
        for part in range(2):
            lane = part * slots
            flat_ref[part : part + 1, b * slots : (b + 1) * slots] = (
                total[b : b + 1, lane : lane + slots]
                + total[far : far + 1, 2 * slots + lane : 2 * slots + lane + slots]
            )
    count = owners * slots
    tall = PIX_OWN // LANES
    pixel = place_ref[...]
    high = lax.broadcasted_iota(jnp.int32, (tall, count), 0) == pixel // LANES
    low = lax.broadcasted_iota(jnp.int32, (LANES, count), 0) == pixel % LANES
    pick_low = low.astype(F32).astype(BF16)
    spread = jnp.concatenate(
        [jnp.where(high, flat_ref[part : part + 1, :], 0.0) for part in range(2)], 0
    )
    coarse = spread.astype(BF16)
    fine = (spread - coarse.astype(F32)).astype(BF16)
    image = dot_nt(coarse, pick_low) + dot_nt(fine, pick_low)
    for part in range(2):
        for h in range(tall):
            row = part * tall + h
            out_ref[part : part + 1, h * LANES : (h + 1) * LANES] = image[row : row + 1, :]


def shape(dims, dtype):
    return jax.ShapeDtypeStruct(dims, dtype)


def call(kernel, out_shape, in_specs, out_specs, flops=0, nbytes=0, scratch=(), grid=None):
    extra = {} if grid is None else {"grid": grid}
    return pl.pallas_call(
        kernel,
        out_shape=out_shape,
        in_specs=in_specs,
        out_specs=out_specs,
        scratch_shapes=list(scratch),
        cost_estimate=pl.CostEstimate(flops=flops, bytes_accessed=nbytes, transcendentals=0),
        compiler_params=pltpu.CompilerParams(vmem_limit_bytes=24 * 2**20),
        **extra,
    )


def whole(array):
    return pl.BlockSpec(array.shape, lambda i: (0,) * array.ndim)


def swapped(value, axis, bit):
    return lax.ppermute(value, axis, [(i, i ^ 1 << bit) for i in range(lax.axis_size(axis))])


def neighbour_edges(edges):
    count = lax.axis_size("rng")
    if count == 2:
        return lax.ppermute(edges, "rng", [(0, 1), (1, 0)])
    half = edges.shape[0] // 2
    after = lax.ppermute(edges[:half], "rng", [(i + 1, i) for i in range(count - 1)])
    before = lax.ppermute(edges[half:], "rng", [(i, i + 1) for i in range(count - 1)])
    return jnp.concatenate([after, before], 0)


def local(raw, filt, steer, chan_w, merge_w, samp_index, samp_weight, counts, pixel_id):
    channels, _, pulses, bins = raw.shape
    size = steer.shape[1]
    levels = merge_w.shape[1]
    taps, owners, slots = samp_index.shape[1:]
    extra = 4 * taps * owners * slots // ROW
    blocks = lax.axis_size("rng")
    rims = channels * 2 * EDGE * (1 if blocks == 2 else 2)
    edges = call(
        functools.partial(rim_kernel, "rng", blocks),
        shape((rims, pulses), BF16),
        [VMEM],
        VMEM,
        flops=2**32,
        nbytes=2**24,
    )(raw)
    beside = neighbour_edges(edges)
    pack = call(
        functools.partial(pack_kernel, bins.bit_length() - 1, "chan"),
        shape((size // 2 + extra, ROW), BF16),
        [VMEM] * 4,
        VMEM,
    )(merge_w, samp_index, samp_weight, counts)
    near = swapped(pack, "sub", levels - 1)
    bands, ends, mix = call(
        functools.partial(filter_kernel, bins, "rng", blocks),
        (
            shape((channels, 2, bins, bins), BF16),
            shape((2 * rims, channels * bins), BF16),
            shape((16 * channels, bins), F32),
        ),
        [VMEM] * 2,
        (VMEM,) * 3,
    )(filt, chan_w)
    main = call(
        image_kernel,
        shape((size, bins), F32),
        [VMEM] * 4,
        VMEM,
        flops=2**30,
        nbytes=2**21,
    )(raw, steer, bands, mix)
    polar = call(
        edge_kernel,
        shape((size, bins), BF16),
        [VMEM] * 5,
        VMEM,
        flops=2**27,
        nbytes=2**20,
    )(main, beside, steer, ends, mix)
    far = swapped(lax.optimization_barrier((polar, near))[1], "chan", 0)
    for level in range(levels - 2):
        other = swapped(polar, "sub", level)
        polar = call(
            merge_kernel,
            shape((size, bins), BF16),
            [
                pl.BlockSpec((1, 1, 2, size, size), lambda i, level=level: (0, level, 0, 0, 0)),
                whole(polar),
                whole(other),
            ],
            pl.BlockSpec((size, bins), lambda i: (0, 0)),
            grid=(1,),
        )(merge_w, polar, other)
    other = swapped(polar, "sub", levels - 2)
    outgoing = call(
        functools.partial(sample_kernel, taps, slots, "chan"),
        shape((2 * owners, 4 * slots), F32),
        [VMEM] * 6,
        VMEM,
        flops=2**28,
        nbytes=2**20,
    )(merge_w[:, levels - 2 :], polar, other, pack, near, far)
    values = lax.all_to_all(
        outgoing, ("chan", "sub", "rng"), split_axis=0, concat_axis=0, tiled=True
    )
    return call(
        scatter_kernel,
        shape((2, PIX_OWN), F32),
        [VMEM, VMEM],
        VMEM,
        scratch=[
            pltpu.VMEM((2, owners * slots), F32),
            pltpu.VMEM((1, owners * slots), jnp.int32),
        ],
    )(values, pixel_id)


def solution(mesh):
    placed = (
        P("chan", None, ("groups", "sub"), "rng"),
        P("chan", None, None),
        P("sub", None, None),
        P("chan", None),
        P("sub", None, None, None, None),
        P(("sub", "rng"), None, None, None),
        P(("sub", "rng"), None, None, None),
        P(("sub", "rng"), None),
        P(("sub", "rng"), None, None),
    )
    return jax.shard_map(
        local,
        mesh=mesh,
        in_specs=placed,
        out_specs=P(None, ("groups", "sub", "rng")),
        check_vma=False,
    )
```

```python
import functools

import jax
import jax.numpy as jnp
from jax import lax
from jax.experimental import pallas as pl
from jax.experimental.pallas import tpu as pltpu
from jax.sharding import PartitionSpec as P

PIX_OWN = 4096
LANES = 128
ROW = 256
EDGE = 8
F32 = jnp.float32
BF16 = jnp.bfloat16
VMEM = pl.BlockSpec(memory_space=pltpu.VMEM)
NT = (((1,), (1,)), ((), ()))


def dot(a, b):
    return jnp.dot(a, b, preferred_element_type=F32)


def dot_nt(a, b):
    return lax.dot_general(a, b, NT, preferred_element_type=F32)


def place_kernel(rng_axis, rng_size, place_ref):
    bins = place_ref.shape[1]
    block = lax.axis_index(rng_axis)
    row = lax.broadcasted_iota(jnp.int32, (2 * EDGE, bins), 0)
    column = lax.broadcasted_iota(jnp.int32, (2 * EDGE, bins), 1)
    after = jnp.where(block < rng_size - 1, bins - EDGE, 2 * bins)
    before = jnp.where(block > 0, -EDGE, 2 * bins)
    here = column == row + jnp.where(row < EDGE, after, before)
    place_ref[...] = here.astype(F32).astype(BF16)


def pack_kernel(
    shift, chan_axis, merge_ref, index_ref, weight_ref, counts_ref, _, pack_ref
):
    half = merge_ref.shape[3] // 2
    last = merge_ref.shape[1] - 1
    core = lax.axis_index(chan_axis) % 2
    rows = pl.ds(pl.multiple_of(core * half, half), half)
    pack_ref[:half, :] = merge_ref[0, last, 1, rows, :]
    taps, owners, slots = index_ref.shape[1:]
    per_row = ROW // slots
    slot = lax.broadcasted_iota(jnp.int32, (taps, slots), 1)
    for first in range(0, owners, per_row):
        index = jnp.concatenate([index_ref[0, :, first + k, :] for k in range(per_row)], 1)
        weight = jnp.concatenate(
            [
                jnp.where(slot < counts_ref[:, first + k : first + k + 1], weight_ref[0, :, first + k, :], 0.0)
                for k in range(per_row)
            ],
            1,
        )
        coarse = weight.astype(BF16).astype(F32)
        beam = (index >> shift).astype(F32)
        column = (index & ((1 << shift) - 1)).astype(F32)
        lines = jnp.concatenate([beam, column, coarse, weight - coarse], 0).astype(BF16)
        base = half + 4 * taps * (first // per_row)
        pack_ref[base : base + 4 * taps, :] = lines


def filter_kernel(bins, filt_ref, chan_ref, band_ref, outer_ref, mix_ref):
    channels, parts, taps = filt_ref.shape
    rows = jnp.concatenate([filt_ref[c] for c in range(channels)], 0).astype(BF16)
    source = lax.broadcasted_iota(jnp.int32, (taps, LANES), 0)
    target = lax.broadcasted_iota(jnp.int32, (taps, LANES), 1)
    mirror = (source == ((EDGE - target) & (LANES - 1))).astype(F32).astype(BF16)
    bases = dot(rows, mirror)
    forward = dot(rows, (source == target).astype(F32).astype(BF16))
    row = lax.broadcasted_iota(jnp.int32, (LANES, LANES), 0)
    column = lax.broadcasted_iota(jnp.int32, (LANES, LANES), 1)
    far = column - row
    zero = jnp.zeros((LANES, LANES), BF16)
    count = bins // LANES
    low = lax.broadcasted_iota(jnp.int32, (EDGE, LANES), 1) < LANES // 2
    blank = jnp.zeros((EDGE, bins - LANES), F32)

    def turning(base, size, shift):
        wide = jnp.broadcast_to(base, (size, LANES))
        return pltpu.roll(wide, shift, 1, stride=1, stride_axis=0)

    for c in range(channels):
        for part in range(parts):
            line = slice(c * parts + part, c * parts + part + 1)
            ring = turning(bases[line], LANES, 0)
            blocks = {
                0: jnp.where((far < 64) & (far > -64), ring, 0.0).astype(BF16),
                1: jnp.where(far >= 64, ring, 0.0).astype(BF16),
                -1: jnp.where(far <= -64, ring, 0.0).astype(BF16),
            }
            for i in range(count):
                for o in range(count):
                    band_ref[
                        c, part, i * LANES : (i + 1) * LANES, o * LANES : (o + 1) * LANES
                    ] = blocks.get(i - o, zero)
            lower = jnp.where(low, turning(forward[line], EDGE, LANES - 2 * EDGE), 0.0)
            upper = jnp.where(low, 0.0, turning(forward[line], EDGE, LANES - EDGE))
            outer = jnp.concatenate(
                [jnp.concatenate([lower, blank], 1), jnp.concatenate([blank, upper], 1)], 0
            )
            outer_ref[c, part] = outer.astype(BF16)
            mix_ref[8 * (2 * c + part) : 8 * (2 * c + part + 1), :] = jnp.broadcast_to(
                chan_ref[c : c + 1, part : part + 1], (8, bins)
            )


def turned(value, mix_ref, channel):
    half = value.shape[0] // 2
    re, im = value[:half], value[half:]
    wr = mix_ref[16 * channel : 16 * channel + 1, :]
    wi = mix_ref[16 * channel + 8 : 16 * channel + 9, :]
    return jnp.concatenate([wr * re - wi * im, wr * im + wi * re], 0)


def image_kernel(raw_ref, steer_ref, band_ref, outer_ref, mix_ref, out_ref, rim_ref):
    channels, _, pulses, _ = raw_ref.shape
    s_re, s_im = steer_ref[0, :, :pulses], steer_ref[0, :, pulses:]
    half = steer_ref.shape[1] // 2
    total = jnp.zeros(out_ref.shape, F32)
    rim = jnp.zeros(rim_ref.shape, F32)
    for c in range(channels):
        x_re, x_im = raw_ref[c, 0], raw_ref[c, 1]
        direct = (dot(s_re, x_re) + dot(s_im, x_im)).astype(BF16)
        cross = (dot(s_im, x_re) - dot(s_re, x_im)).astype(BF16)
        image = dot(direct, band_ref[c, 0]) + dot(cross, band_ref[c, 1])
        total = total + turned(image, mix_ref, c)
        side = dot_nt(outer_ref[c, 0], direct) + dot_nt(outer_ref[c, 1], cross)
        re, im = side[:, :half], side[:, half:]
        wr = mix_ref[16 * c : 16 * c + 1, :half]
        wi = mix_ref[16 * c + 8 : 16 * c + 9, :half]
        rim = rim + jnp.concatenate([wr * re - wi * im, wr * im + wi * re], 1)
    out_ref[...] = total.astype(BF16)
    rim_ref[...] = rim.astype(BF16)


def spread_rim(rim_ref, place_ref):
    return lax.dot_general(
        rim_ref[...], place_ref[...], (((0,), (0,)), ((), ())), preferred_element_type=F32
    )


def whole_kernel(main_ref, rim_ref, place_ref, out_ref):
    added = spread_rim(rim_ref, place_ref)
    out_ref[...] = (main_ref[...].astype(F32) + added).astype(BF16)


def merge_kernel(weight_ref, own_ref, other_ref, out_ref):
    mixed = dot(weight_ref[0, 0, 0], own_ref[...]) + dot(weight_ref[0, 0, 1], other_ref[...])
    out_ref[...] = mixed.astype(BF16)


def slot_masks(ref, base, t, taps, bins, half):
    rows = ref[base : base + 4 * taps, :].astype(F32)
    beam = rows[t : t + 1]
    column = rows[taps + t : taps + t + 1]
    weight = rows[2 * taps + t : 2 * taps + t + 1] + rows[3 * taps + t : 3 * taps + t + 1]
    bin_ids = lax.broadcasted_iota(jnp.int32, (bins, ROW), 0).astype(F32)
    beam_ids = lax.broadcasted_iota(jnp.int32, (half, ROW), 0).astype(F32)
    pick_bin = (bin_ids == column).astype(F32).astype(BF16)
    return pick_bin, jnp.where(beam_ids == beam, weight, 0.0)


def mixed_kernel(weight_ref, own_ref, own_rim_ref, other_rim_ref, place_ref, mixed_ref):
    own = (own_ref[...].astype(F32) + spread_rim(own_rim_ref, place_ref)).astype(BF16)
    other = spread_rim(other_rim_ref, place_ref).astype(BF16)
    mixed_ref[...] = dot(weight_ref[0, 0, 0], own) + dot(weight_ref[0, 0, 1], other)


def ready_kernel(taps, pack_ref, near_ref, pixel_ref, _, low_ref, high_ref, bin_ref, beam_ref):
    half, bins = beam_ref.shape[1], bin_ref.shape[1]
    owners, slots = pixel_ref.shape[1:]
    for block, ref in enumerate((pack_ref, near_ref)):
        for t in range(taps):
            pick_bin, pick_beam = slot_masks(ref, half, t, taps, bins, half)
            bin_ref[block * taps + t] = pick_bin
            beam_ref[block * taps + t] = pick_beam
    pixel = jnp.concatenate([pixel_ref[0, b : b + 1, :] for b in range(owners)], 1)
    count = owners * slots
    low = lax.broadcasted_iota(jnp.int32, (LANES, count), 0) == (pixel & (LANES - 1))
    low_ref[...] = low.astype(F32).astype(BF16)
    tall = high_ref.shape[0]
    high = lax.broadcasted_iota(jnp.int32, (tall, count), 0) == pixel // LANES
    high_ref[...] = high.astype(F32)


def sample_kernel(
    taps, slots, chan_axis, weight_ref, mixed_ref, other_ref, pack_ref, near_ref, far_ref, *refs
):
    ready, out_ref = refs[:-1], refs[-1]
    size, bins = other_ref.shape
    half = size // 2
    mixed = mixed_ref[...] + dot(weight_ref[0, 0, 1], other_ref[...])
    polar = mixed.astype(BF16)
    chunks = (pack_ref.shape[0] - half) // (4 * taps)
    per_row = ROW // slots
    owners = per_row * chunks
    even = lax.axis_index(chan_axis) % 2 == 0
    far = jnp.concatenate([near_ref[:half, :], far_ref[:half, :]], 0)
    values = {}
    for block, (merge, ref) in enumerate(((weight_ref[0, 1, 0], pack_ref), (far, near_ref))):
        merged = dot(merge, polar).astype(BF16)
        for chunk in range(chunks):
            base = half + 4 * taps * chunk
            sums = [jnp.zeros((half, ROW), F32) for _ in range(2)]
            for t in range(taps):
                if ready:
                    pick_bin = ready[0][block * taps + t]
                    pick_beam = ready[1][block * taps + t]
                else:
                    pick_bin, pick_beam = slot_masks(ref, base, t, taps, bins, half)
                found = dot(merged, pick_bin)
                sums[0] = sums[0] + found[:half] * pick_beam
                sums[1] = sums[1] + found[half:] * pick_beam
            flat = [jnp.sum(value, axis=0, keepdims=True) for value in sums]
            if block == 1:
                flat = [jnp.where(even, flat[0], flat[1]), jnp.where(even, flat[1], flat[0])]
            values[chunk] = values.get(chunk, []) + flat
    for chunk in range(chunks):
        rows = [
            jnp.concatenate([v[:, k * slots : (k + 1) * slots] for v in values[chunk]], 1)
            for k in range(per_row)
        ]
        tile = jnp.concatenate(rows, 0)
        for copy in range(2):
            top = copy * owners + chunk * per_row
            out_ref[top : top + per_row, :] = tile


def scatter_kernel(slots, value_ref, low_ref, high_ref, out_ref):
    owners = value_ref.shape[0] // 2
    total = value_ref[:owners, :] + value_ref[owners:, :]
    flat = []
    for part in range(2):
        lane = part * slots
        own = total[:, lane : lane + slots]
        far = total[:, 2 * slots + lane : 2 * slots + lane + slots]
        far = jnp.concatenate([far[owners // 2 :], far[: owners // 2]], 0)
        both = own + far
        flat.append(jnp.concatenate([both[b : b + 1] for b in range(owners)], 1))
    high = high_ref[...]
    tall = high.shape[0]
    spread = jnp.concatenate([high * flat[part] for part in range(2)], 0)
    coarse = spread.astype(BF16)
    fine = (spread - coarse.astype(F32)).astype(BF16)
    low = low_ref[...]
    image = dot_nt(coarse, low) + dot_nt(fine, low)
    for part in range(2):
        for h in range(tall):
            row = part * tall + h
            out_ref[part : part + 1, h * LANES : (h + 1) * LANES] = image[row : row + 1, :]


def shape(dims, dtype):
    return jax.ShapeDtypeStruct(dims, dtype)


def call(kernel, out_shape, in_specs, out_specs, flops=0, nbytes=0, scratch=(), grid=None):
    extra = {} if grid is None else {"grid": grid}
    return pl.pallas_call(
        kernel,
        out_shape=out_shape,
        in_specs=in_specs,
        out_specs=out_specs,
        scratch_shapes=list(scratch),
        cost_estimate=pl.CostEstimate(flops=flops, bytes_accessed=nbytes, transcendentals=0),
        compiler_params=pltpu.CompilerParams(vmem_limit_bytes=24 * 2**20),
        **extra,
    )


def whole(array):
    return pl.BlockSpec(array.shape, lambda i: (0,) * array.ndim)


def swapped(value, axis, bit):
    return lax.ppermute(value, axis, [(i, i ^ 1 << bit) for i in range(lax.axis_size(axis))])


def neighbour_rims(rim):
    count = lax.axis_size("rng")
    if count == 2:
        return lax.ppermute(rim, "rng", [(0, 1), (1, 0)])
    after = lax.ppermute(rim, "rng", [(i + 1, i) for i in range(count - 1)])
    before = lax.ppermute(rim, "rng", [(i, i + 1) for i in range(count - 1)])
    return jnp.concatenate([after[:EDGE], before[EDGE:]], 0)


def local(raw, filt, steer, chan_w, merge_w, samp_index, samp_weight, counts, pixel_id):
    channels, _, pulses, bins = raw.shape
    size = steer.shape[1]
    levels = merge_w.shape[1]
    taps, owners, slots = samp_index.shape[1:]
    extra = 4 * taps * owners * slots // ROW
    blocks = lax.axis_size("rng")
    place = call(
        functools.partial(place_kernel, "rng", blocks),
        shape((2 * EDGE, bins), BF16),
        [],
        VMEM,
        flops=2**32,
        nbytes=2**24,
    )()
    pack = call(
        functools.partial(pack_kernel, bins.bit_length() - 1, "chan"),
        shape((size // 2 + extra, ROW), BF16),
        [VMEM] * 5,
        VMEM,
    )(merge_w, samp_index, samp_weight, counts, place)
    near = swapped(pack, "sub", levels - 1)
    bands, outer, mix = call(
        functools.partial(filter_kernel, bins),
        (
            shape((channels, 2, bins, bins), BF16),
            shape((channels, 2, 2 * EDGE, bins), BF16),
            shape((16 * channels, bins), F32),
        ),
        [VMEM] * 2,
        (VMEM,) * 3,
    )(filt, chan_w)
    main, rim = call(
        image_kernel,
        (shape((size, bins), BF16), shape((2 * EDGE, size), BF16)),
        [VMEM] * 5,
        (VMEM,) * 2,
        flops=2**30,
        nbytes=2**21,
    )(raw, steer, bands, outer, mix)
    polar, own_rim = main, neighbour_rims(rim)
    if levels == 2 and blocks == 2:
        groups = lax.axis_size("sub") * blocks
        other_rim = lax.ppermute(rim, ("sub", "rng"), [(i, i ^ 3) for i in range(groups)])
    else:
        polar = call(whole_kernel, shape((size, bins), BF16), [VMEM] * 3, VMEM)(
            main, own_rim, place
        )
        own_rim = other_rim = jnp.zeros((2 * EDGE, size), BF16)
    far = swapped(lax.optimization_barrier((polar, near))[1], "chan", 0)
    for level in range(levels - 2):
        other = swapped(polar, "sub", level)
        polar = call(
            merge_kernel,
            shape((size, bins), BF16),
            [
                pl.BlockSpec((1, 1, 2, size, size), lambda i, level=level: (0, level, 0, 0, 0)),
                whole(polar),
                whole(other),
            ],
            pl.BlockSpec((size, bins), lambda i: (0, 0)),
            grid=(1,),
        )(merge_w, polar, other)
    other = swapped(polar, "sub", levels - 2)
    chunks = owners * slots // ROW
    tall = PIX_OWN // LANES
    count = owners * slots
    sets = 2 * taps
    weights = merge_w[:, levels - 2 :]
    mixed = call(mixed_kernel, shape((size, bins), F32), [VMEM] * 5, VMEM, flops=2**31, nbytes=2**20)(
        weights, polar, own_rim, other_rim, place
    )
    low, high, *ready = call(
        functools.partial(ready_kernel, taps),
        (
            shape((LANES, count), BF16),
            shape((tall, count), F32),
            shape((sets, bins, ROW), BF16),
            shape((sets, size // 2, ROW), F32),
        ),
        [VMEM] * 4,
        (VMEM,) * 4,
        flops=2**27,
        nbytes=2**19,
    )(pack, near, pixel_id, mixed)
    if chunks > 1:
        ready = []
    outgoing = call(
        functools.partial(sample_kernel, taps, slots, "chan"),
        shape((2 * owners, 4 * slots), F32),
        [VMEM] * (6 + len(ready)),
        VMEM,
        flops=2**28,
        nbytes=2**20,
    )(weights, mixed, other, pack, near, far, *ready)
    values = lax.all_to_all(
        outgoing, ("chan", "sub", "rng"), split_axis=0, concat_axis=0, tiled=True
    )
    return call(
        functools.partial(scatter_kernel, slots), shape((2, PIX_OWN), F32), [VMEM] * 3, VMEM
    )(values, low, high)


def solution(mesh):
    placed = (
        P("chan", None, ("groups", "sub"), "rng"),
        P("chan", None, None),
        P("sub", None, None),
        P("chan", None),
        P("sub", None, None, None, None),
        P(("sub", "rng"), None, None, None),
        P(("sub", "rng"), None, None, None),
        P(("sub", "rng"), None),
        P(("sub", "rng"), None, None),
    )
    return jax.shard_map(
        local,
        mesh=mesh,
        in_specs=placed,
        out_specs=P(None, ("groups", "sub", "rng")),
        check_vma=False,
    )
```

```python
import functools

import jax
import jax.numpy as jnp
from jax import lax
from jax.experimental import pallas as pl
from jax.experimental.pallas import tpu as pltpu
from jax.sharding import PartitionSpec as P

PIX_OWN = 4096
LANES = 128
ROW = 256
EDGE = 8
F32 = jnp.float32
BF16 = jnp.bfloat16
VMEM = pl.BlockSpec(memory_space=pltpu.VMEM)
NT = (((1,), (1,)), ((), ()))


def dot(a, b):
    return jnp.dot(a, b, preferred_element_type=F32)


def dot_nt(a, b):
    return lax.dot_general(a, b, NT, preferred_element_type=F32)


def place_kernel(rng_axis, rng_size, place_ref):
    bins = place_ref.shape[1]
    block = lax.axis_index(rng_axis)
    row = lax.broadcasted_iota(jnp.int32, (2 * EDGE, bins), 0)
    column = lax.broadcasted_iota(jnp.int32, (2 * EDGE, bins), 1)
    after = jnp.where(block < rng_size - 1, bins - EDGE, 2 * bins)
    before = jnp.where(block > 0, -EDGE, 2 * bins)
    here = column == row + jnp.where(row < EDGE, after, before)
    place_ref[...] = here.astype(F32).astype(BF16)


def pack_kernel(
    shift, chan_axis, merge_ref, index_ref, weight_ref, counts_ref, _first, _filt, _mix, pack_ref
):
    half = merge_ref.shape[3] // 2
    last = merge_ref.shape[1] - 1
    core = lax.axis_index(chan_axis) % 2
    rows = pl.ds(pl.multiple_of(core * half, half), half)
    pack_ref[:half, :] = merge_ref[0, last, 1, rows, :]
    taps, owners, slots = index_ref.shape[1:]
    per_row = ROW // slots
    slot = lax.broadcasted_iota(jnp.int32, (taps, slots), 1)
    for first in range(0, owners, per_row):
        index = jnp.concatenate([index_ref[0, :, first + k, :] for k in range(per_row)], 1)
        weight = jnp.concatenate(
            [
                jnp.where(slot < counts_ref[:, first + k : first + k + 1], weight_ref[0, :, first + k, :], 0.0)
                for k in range(per_row)
            ],
            1,
        )
        coarse = weight.astype(BF16).astype(F32)
        beam = (index >> shift).astype(F32)
        column = (index & ((1 << shift) - 1)).astype(F32)
        lines = jnp.concatenate([beam, column, coarse, weight - coarse], 0).astype(BF16)
        base = half + 4 * taps * (first // per_row)
        pack_ref[base : base + 4 * taps, :] = lines


def filter_kernel(bins, filt_ref, chan_ref, band_ref, outer_ref, mix_ref):
    channels, parts, taps = filt_ref.shape
    rows = jnp.concatenate([filt_ref[c] for c in range(channels)], 0).astype(BF16)
    source = lax.broadcasted_iota(jnp.int32, (taps, LANES), 0)
    target = lax.broadcasted_iota(jnp.int32, (taps, LANES), 1)
    mirror = (source == ((EDGE - target) & (LANES - 1))).astype(F32).astype(BF16)
    bases = dot(rows, mirror)
    forward = dot(rows, (source == target).astype(F32).astype(BF16))
    row = lax.broadcasted_iota(jnp.int32, (LANES, LANES), 0)
    column = lax.broadcasted_iota(jnp.int32, (LANES, LANES), 1)
    far = column - row
    zero = jnp.zeros((LANES, LANES), BF16)
    count = bins // LANES
    low = lax.broadcasted_iota(jnp.int32, (EDGE, LANES), 1) < LANES // 2
    blank = jnp.zeros((EDGE, bins - LANES), F32)

    def turning(base, size, shift):
        wide = jnp.broadcast_to(base, (size, LANES))
        return pltpu.roll(wide, shift, 1, stride=1, stride_axis=0)

    for c in range(channels):
        for part in range(parts):
            line = slice(c * parts + part, c * parts + part + 1)
            ring = turning(bases[line], LANES, 0)
            blocks = {
                0: jnp.where((far < 64) & (far > -64), ring, 0.0).astype(BF16),
                1: jnp.where(far >= 64, ring, 0.0).astype(BF16),
                -1: jnp.where(far <= -64, ring, 0.0).astype(BF16),
            }
            for i in range(count):
                for o in range(count):
                    band_ref[
                        c, part, i * LANES : (i + 1) * LANES, o * LANES : (o + 1) * LANES
                    ] = blocks.get(i - o, zero)
            lower = jnp.where(low, turning(forward[line], EDGE, LANES - 2 * EDGE), 0.0)
            upper = jnp.where(low, 0.0, turning(forward[line], EDGE, LANES - EDGE))
            outer = jnp.concatenate(
                [jnp.concatenate([lower, blank], 1), jnp.concatenate([blank, upper], 1)], 0
            )
            outer_ref[c, part] = outer.astype(BF16)
            mix_ref[8 * (2 * c + part) : 8 * (2 * c + part + 1), :] = jnp.broadcast_to(
                chan_ref[c : c + 1, part : part + 1], (8, bins)
            )


def turned(value, mix_ref, channel):
    half = value.shape[0] // 2
    re, im = value[:half], value[half:]
    wr = mix_ref[16 * channel : 16 * channel + 1, :]
    wi = mix_ref[16 * channel + 8 : 16 * channel + 9, :]
    return jnp.concatenate([wr * re - wi * im, wr * im + wi * re], 0)


def image_kernel(raw_ref, steer_ref, band_ref, outer_ref, mix_ref, out_ref, rim_ref):
    channels, _, pulses, _ = raw_ref.shape
    s_re, s_im = steer_ref[0, :, :pulses], steer_ref[0, :, pulses:]
    half = steer_ref.shape[1] // 2
    total = jnp.zeros(out_ref.shape, F32)
    rim = jnp.zeros(rim_ref.shape, F32)
    for c in range(channels):
        x_re, x_im = raw_ref[c, 0], raw_ref[c, 1]
        direct = (dot(s_re, x_re) + dot(s_im, x_im)).astype(BF16)
        cross = (dot(s_im, x_re) - dot(s_re, x_im)).astype(BF16)
        image = dot(direct, band_ref[c, 0]) + dot(cross, band_ref[c, 1])
        total = total + turned(image, mix_ref, c)
        side = dot_nt(outer_ref[c, 0], direct) + dot_nt(outer_ref[c, 1], cross)
        re, im = side[:, :half], side[:, half:]
        wr = mix_ref[16 * c : 16 * c + 1, :half]
        wi = mix_ref[16 * c + 8 : 16 * c + 9, :half]
        rim = rim + jnp.concatenate([wr * re - wi * im, wr * im + wi * re], 1)
    out_ref[...] = total.astype(BF16)
    rim_ref[...] = rim.astype(BF16)


def spread_rim(rim_ref, place_ref):
    return lax.dot_general(
        rim_ref[...], place_ref[...], (((0,), (0,)), ((), ())), preferred_element_type=F32
    )


def whole_kernel(main_ref, rim_ref, place_ref, out_ref):
    added = spread_rim(rim_ref, place_ref)
    out_ref[...] = (main_ref[...].astype(F32) + added).astype(BF16)


def merge_kernel(weight_ref, own_ref, other_ref, out_ref):
    mixed = dot(weight_ref[0, 0, 0], own_ref[...]) + dot(weight_ref[0, 0, 1], other_ref[...])
    out_ref[...] = mixed.astype(BF16)


def slot_masks(ref, base, t, taps, bins, half):
    rows = ref[base : base + 4 * taps, :].astype(F32)
    beam = rows[t : t + 1]
    column = rows[taps + t : taps + t + 1]
    weight = rows[2 * taps + t : 2 * taps + t + 1] + rows[3 * taps + t : 3 * taps + t + 1]
    bin_ids = lax.broadcasted_iota(jnp.int32, (bins, ROW), 0).astype(F32)
    beam_ids = lax.broadcasted_iota(jnp.int32, (half, ROW), 0).astype(F32)
    pick_bin = (bin_ids == column).astype(F32).astype(BF16)
    return pick_bin, jnp.where(beam_ids == beam, weight, 0.0)


def mixed_kernel(weight_ref, own_ref, own_rim_ref, other_rim_ref, place_ref, _, mixed_ref):
    own = (own_ref[...].astype(F32) + spread_rim(own_rim_ref, place_ref)).astype(BF16)
    other = spread_rim(other_rim_ref, place_ref).astype(BF16)
    mixed_ref[...] = dot(weight_ref[0, 0, 0], own) + dot(weight_ref[0, 0, 1], other)


def ready_kernel(taps, pack_ref, near_ref, pixel_ref, low_ref, high_ref, bin_ref, beam_ref):
    half, bins = beam_ref.shape[1], bin_ref.shape[1]
    owners, slots = pixel_ref.shape[1:]
    for block, ref in enumerate((pack_ref, near_ref)):
        for t in range(taps):
            pick_bin, pick_beam = slot_masks(ref, half, t, taps, bins, half)
            bin_ref[block * taps + t] = pick_bin
            beam_ref[block * taps + t] = pick_beam
    pixel = jnp.concatenate([pixel_ref[0, b : b + 1, :] for b in range(owners)], 1)
    count = owners * slots
    low = lax.broadcasted_iota(jnp.int32, (LANES, count), 0) == (pixel & (LANES - 1))
    low_ref[...] = low.astype(F32).astype(BF16)
    tall = high_ref.shape[0]
    high = lax.broadcasted_iota(jnp.int32, (tall, count), 0) == pixel // LANES
    high_ref[...] = high.astype(F32)


def sample_kernel(
    taps, slots, chan_axis, weight_ref, mixed_ref, other_ref, pack_ref, near_ref, far_ref, *refs
):
    ready, out_ref = refs[:-1], refs[-1]
    size, bins = other_ref.shape
    half = size // 2
    mixed = mixed_ref[...] + dot(weight_ref[0, 0, 1], other_ref[...])
    polar = mixed.astype(BF16)
    chunks = (pack_ref.shape[0] - half) // (4 * taps)
    per_row = ROW // slots
    owners = per_row * chunks
    even = lax.axis_index(chan_axis) % 2 == 0
    far = jnp.concatenate([near_ref[:half, :], far_ref[:half, :]], 0)
    values = {}
    for block, (merge, ref) in enumerate(((weight_ref[0, 1, 0], pack_ref), (far, near_ref))):
        merged = dot(merge, polar).astype(BF16)
        for chunk in range(chunks):
            base = half + 4 * taps * chunk
            sums = [jnp.zeros((half, ROW), F32) for _ in range(2)]
            for t in range(taps):
                if ready:
                    pick_bin = ready[0][block * taps + t]
                    pick_beam = ready[1][block * taps + t]
                else:
                    pick_bin, pick_beam = slot_masks(ref, base, t, taps, bins, half)
                found = dot(merged, pick_bin)
                sums[0] = sums[0] + found[:half] * pick_beam
                sums[1] = sums[1] + found[half:] * pick_beam
            flat = [jnp.sum(value, axis=0, keepdims=True) for value in sums]
            if block == 1:
                flat = [jnp.where(even, flat[0], flat[1]), jnp.where(even, flat[1], flat[0])]
            values[chunk] = values.get(chunk, []) + flat
    for chunk in range(chunks):
        rows = [
            jnp.concatenate([v[:, k * slots : (k + 1) * slots] for v in values[chunk]], 1)
            for k in range(per_row)
        ]
        tile = jnp.concatenate(rows, 0)
        for copy in range(2):
            top = copy * owners + chunk * per_row
            out_ref[top : top + per_row, :] = tile


def scatter_kernel(slots, value_ref, low_ref, high_ref, out_ref):
    owners = value_ref.shape[0] // 2
    total = value_ref[:owners, :] + value_ref[owners:, :]
    flat = []
    for part in range(2):
        lane = part * slots
        own = total[:, lane : lane + slots]
        far = total[:, 2 * slots + lane : 2 * slots + lane + slots]
        far = jnp.concatenate([far[owners // 2 :], far[: owners // 2]], 0)
        both = own + far
        flat.append(jnp.concatenate([both[b : b + 1] for b in range(owners)], 1))
    high = high_ref[...]
    tall = high.shape[0]
    spread = jnp.concatenate([high * flat[part] for part in range(2)], 0)
    coarse = spread.astype(BF16)
    fine = (spread - coarse.astype(F32)).astype(BF16)
    low = low_ref[...]
    image = dot_nt(coarse, low) + dot_nt(fine, low)
    for part in range(2):
        for h in range(tall):
            row = part * tall + h
            out_ref[part : part + 1, h * LANES : (h + 1) * LANES] = image[row : row + 1, :]


def shape(dims, dtype):
    return jax.ShapeDtypeStruct(dims, dtype)


def call(kernel, out_shape, in_specs, out_specs, flops=0, nbytes=0, scratch=(), grid=None):
    extra = {} if grid is None else {"grid": grid}
    return pl.pallas_call(
        kernel,
        out_shape=out_shape,
        in_specs=in_specs,
        out_specs=out_specs,
        scratch_shapes=list(scratch),
        cost_estimate=pl.CostEstimate(flops=flops, bytes_accessed=nbytes, transcendentals=0),
        compiler_params=pltpu.CompilerParams(vmem_limit_bytes=24 * 2**20),
        **extra,
    )


def whole(array):
    return pl.BlockSpec(array.shape, lambda i: (0,) * array.ndim)


def swapped(value, axis, bit):
    return lax.ppermute(value, axis, [(i, i ^ 1 << bit) for i in range(lax.axis_size(axis))])


def neighbour_rims(rim):
    count = lax.axis_size("rng")
    if count == 2:
        return lax.ppermute(rim, "rng", [(0, 1), (1, 0)])
    after = lax.ppermute(rim, "rng", [(i + 1, i) for i in range(count - 1)])
    before = lax.ppermute(rim, "rng", [(i, i + 1) for i in range(count - 1)])
    return jnp.concatenate([after[:EDGE], before[EDGE:]], 0)


def local(raw, filt, steer, chan_w, merge_w, samp_index, samp_weight, counts, pixel_id):
    channels, _, pulses, bins = raw.shape
    size = steer.shape[1]
    levels = merge_w.shape[1]
    taps, owners, slots = samp_index.shape[1:]
    extra = 4 * taps * owners * slots // ROW
    blocks = lax.axis_size("rng")
    place = call(
        functools.partial(place_kernel, "rng", blocks),
        shape((2 * EDGE, bins), BF16),
        [],
        VMEM,
        flops=2**32,
        nbytes=2**24,
    )()
    pack = call(
        functools.partial(pack_kernel, bins.bit_length() - 1, "chan"),
        shape((size // 2 + extra, ROW), BF16),
        [VMEM] * 7,
        VMEM,
    )(merge_w, samp_index, samp_weight, counts, place, filt, chan_w)
    near = swapped(pack, "sub", levels - 1)
    bands, outer, mix = call(
        functools.partial(filter_kernel, bins),
        (
            shape((channels, 2, bins, bins), BF16),
            shape((channels, 2, 2 * EDGE, bins), BF16),
            shape((16 * channels, bins), F32),
        ),
        [VMEM] * 2,
        (VMEM,) * 3,
    )(filt, chan_w)
    main, rim = call(
        image_kernel,
        (shape((size, bins), BF16), shape((2 * EDGE, size), BF16)),
        [VMEM] * 5,
        (VMEM,) * 2,
        flops=2**30,
        nbytes=2**21,
    )(raw, steer, bands, outer, mix)
    polar, own_rim = main, neighbour_rims(rim)
    if levels == 2 and blocks == 2:
        groups = lax.axis_size("sub") * blocks
        other_rim = lax.ppermute(rim, ("sub", "rng"), [(i, i ^ 3) for i in range(groups)])
    else:
        polar = call(whole_kernel, shape((size, bins), BF16), [VMEM] * 3, VMEM)(
            main, own_rim, place
        )
        own_rim = other_rim = jnp.zeros((2 * EDGE, size), BF16)
    far = swapped(lax.optimization_barrier((polar, near))[1], "chan", 0)
    for level in range(levels - 2):
        other = swapped(polar, "sub", level)
        polar = call(
            merge_kernel,
            shape((size, bins), BF16),
            [
                pl.BlockSpec((1, 1, 2, size, size), lambda i, level=level: (0, level, 0, 0, 0)),
                whole(polar),
                whole(other),
            ],
            pl.BlockSpec((size, bins), lambda i: (0, 0)),
            grid=(1,),
        )(merge_w, polar, other)
    other = swapped(polar, "sub", levels - 2)
    chunks = owners * slots // ROW
    tall = PIX_OWN // LANES
    count = owners * slots
    sets = 2 * taps
    weights = merge_w[:, levels - 2 :]
    low, high, *ready = call(
        functools.partial(ready_kernel, taps),
        (
            shape((LANES, count), BF16),
            shape((tall, count), F32),
            shape((sets, bins, ROW), BF16),
            shape((sets, size // 2, ROW), F32),
        ),
        [VMEM] * 3,
        (VMEM,) * 4,
        flops=2**27,
        nbytes=2**19,
    )(pack, near, pixel_id)
    mixed = call(mixed_kernel, shape((size, bins), F32), [VMEM] * 6, VMEM, flops=2**30, nbytes=2**18)(
        weights, polar, own_rim, other_rim, place, high
    )
    if chunks > 1:
        ready = []
    outgoing = call(
        functools.partial(sample_kernel, taps, slots, "chan"),
        shape((2 * owners, 4 * slots), F32),
        [VMEM] * (6 + len(ready)),
        VMEM,
        flops=2**28,
        nbytes=2**20,
    )(weights, mixed, other, pack, near, far, *ready)
    values = lax.all_to_all(
        outgoing, ("chan", "sub", "rng"), split_axis=0, concat_axis=0, tiled=True
    )
    return call(
        functools.partial(scatter_kernel, slots), shape((2, PIX_OWN), F32), [VMEM] * 3, VMEM
    )(values, low, high)


def solution(mesh):
    placed = (
        P("chan", None, ("groups", "sub"), "rng"),
        P("chan", None, None),
        P("sub", None, None),
        P("chan", None),
        P("sub", None, None, None, None),
        P(("sub", "rng"), None, None, None),
        P(("sub", "rng"), None, None, None),
        P(("sub", "rng"), None),
        P(("sub", "rng"), None, None),
    )
    return jax.shard_map(
        local,
        mesh=mesh,
        in_specs=placed,
        out_specs=P(None, ("groups", "sub", "rng")),
        check_vma=False,
    )
```

```python
import functools

import jax
import jax.numpy as jnp
from jax import lax
from jax.experimental import pallas as pl
from jax.experimental.pallas import tpu as pltpu
from jax.sharding import PartitionSpec as P

PIX_OWN = 4096
LANES = 128
ROW = 256
EDGE = 8
F32 = jnp.float32
BF16 = jnp.bfloat16
VMEM = pl.BlockSpec(memory_space=pltpu.VMEM)
NT = (((1,), (1,)), ((), ()))


def dot(a, b):
    return jnp.dot(a, b, preferred_element_type=F32)


def dot_nt(a, b):
    return lax.dot_general(a, b, NT, preferred_element_type=F32)


def place_kernel(rng_axis, rng_size, place_ref):
    bins = place_ref.shape[1]
    block = lax.axis_index(rng_axis)
    row = lax.broadcasted_iota(jnp.int32, (2 * EDGE, bins), 0)
    column = lax.broadcasted_iota(jnp.int32, (2 * EDGE, bins), 1)
    after = jnp.where(block < rng_size - 1, bins - EDGE, 2 * bins)
    before = jnp.where(block > 0, -EDGE, 2 * bins)
    here = column == row + jnp.where(row < EDGE, after, before)
    place_ref[...] = here.astype(F32).astype(BF16)


def pack_kernel(
    shift, chan_axis, merge_ref, index_ref, weight_ref, counts_ref, _first, _filt, _mix, pack_ref
):
    half = merge_ref.shape[3] // 2
    last = merge_ref.shape[1] - 1
    core = lax.axis_index(chan_axis) % 2
    rows = pl.ds(pl.multiple_of(core * half, half), half)
    pack_ref[:half, :] = merge_ref[0, last, 1, rows, :]
    taps, owners, slots = index_ref.shape[1:]
    per_row = ROW // slots
    slot = lax.broadcasted_iota(jnp.int32, (taps, slots), 1)
    for first in range(0, owners, per_row):
        index = jnp.concatenate([index_ref[0, :, first + k, :] for k in range(per_row)], 1)
        weight = jnp.concatenate(
            [
                jnp.where(slot < counts_ref[:, first + k : first + k + 1], weight_ref[0, :, first + k, :], 0.0)
                for k in range(per_row)
            ],
            1,
        )
        coarse = weight.astype(BF16).astype(F32)
        beam = (index >> shift).astype(F32)
        column = (index & ((1 << shift) - 1)).astype(F32)
        lines = jnp.concatenate([beam, column, coarse, weight - coarse], 0).astype(BF16)
        base = half + 4 * taps * (first // per_row)
        pack_ref[base : base + 4 * taps, :] = lines


def filter_kernel(bins, filt_ref, chan_ref, band_ref, outer_ref, mix_ref):
    channels, parts, taps = filt_ref.shape
    rows = jnp.concatenate([filt_ref[c] for c in range(channels)], 0).astype(BF16)
    source = lax.broadcasted_iota(jnp.int32, (taps, LANES), 0)
    target = lax.broadcasted_iota(jnp.int32, (taps, LANES), 1)
    mirror = (source == ((EDGE - target) & (LANES - 1))).astype(F32).astype(BF16)
    bases = dot(rows, mirror)
    forward = dot(rows, (source == target).astype(F32).astype(BF16))
    row = lax.broadcasted_iota(jnp.int32, (LANES, LANES), 0)
    column = lax.broadcasted_iota(jnp.int32, (LANES, LANES), 1)
    far = column - row
    zero = jnp.zeros((LANES, LANES), BF16)
    count = bins // LANES
    low = lax.broadcasted_iota(jnp.int32, (EDGE, LANES), 1) < LANES // 2
    blank = jnp.zeros((EDGE, bins - LANES), F32)

    def turning(base, size, shift):
        wide = jnp.broadcast_to(base, (size, LANES))
        return pltpu.roll(wide, shift, 1, stride=1, stride_axis=0)

    for c in range(channels):
        for part in range(parts):
            line = slice(c * parts + part, c * parts + part + 1)
            ring = turning(bases[line], LANES, 0)
            blocks = {
                0: jnp.where((far < 64) & (far > -64), ring, 0.0).astype(BF16),
                1: jnp.where(far >= 64, ring, 0.0).astype(BF16),
                -1: jnp.where(far <= -64, ring, 0.0).astype(BF16),
            }
            for i in range(count):
                for o in range(count):
                    band_ref[
                        c, part, i * LANES : (i + 1) * LANES, o * LANES : (o + 1) * LANES
                    ] = blocks.get(i - o, zero)
            lower = jnp.where(low, turning(forward[line], EDGE, LANES - 2 * EDGE), 0.0)
            upper = jnp.where(low, 0.0, turning(forward[line], EDGE, LANES - EDGE))
            outer = jnp.concatenate(
                [jnp.concatenate([lower, blank], 1), jnp.concatenate([blank, upper], 1)], 0
            )
            outer_ref[c, part] = outer.astype(BF16)
            mix_ref[8 * (2 * c + part) : 8 * (2 * c + part + 1), :] = jnp.broadcast_to(
                chan_ref[c : c + 1, part : part + 1], (8, bins)
            )


def turned(value, mix_ref, channel):
    half = value.shape[0] // 2
    re, im = value[:half], value[half:]
    wr = mix_ref[16 * channel : 16 * channel + 1, :]
    wi = mix_ref[16 * channel + 8 : 16 * channel + 9, :]
    return jnp.concatenate([wr * re - wi * im, wr * im + wi * re], 0)


def image_kernel(raw_ref, steer_ref, band_ref, outer_ref, mix_ref, out_ref, rim_ref):
    channels, _, pulses, _ = raw_ref.shape
    s_re, s_im = steer_ref[0, :, :pulses], steer_ref[0, :, pulses:]
    half = steer_ref.shape[1] // 2
    total = jnp.zeros(out_ref.shape, F32)
    rim = jnp.zeros(rim_ref.shape, F32)
    for c in range(channels):
        x_re, x_im = raw_ref[c, 0], raw_ref[c, 1]
        direct = (dot(s_re, x_re) + dot(s_im, x_im)).astype(BF16)
        cross = (dot(s_im, x_re) - dot(s_re, x_im)).astype(BF16)
        image = dot(direct, band_ref[c, 0]) + dot(cross, band_ref[c, 1])
        total = total + turned(image, mix_ref, c)
        side = dot_nt(outer_ref[c, 0], direct) + dot_nt(outer_ref[c, 1], cross)
        re, im = side[:, :half], side[:, half:]
        wr = mix_ref[16 * c : 16 * c + 1, :half]
        wi = mix_ref[16 * c + 8 : 16 * c + 9, :half]
        rim = rim + jnp.concatenate([wr * re - wi * im, wr * im + wi * re], 1)
    out_ref[...] = total.astype(BF16)
    rim_ref[...] = rim.astype(BF16)


def spread_rim(rim_ref, place_ref):
    return lax.dot_general(
        rim_ref[...], place_ref[...], (((0,), (0,)), ((), ())), preferred_element_type=F32
    )


def whole_kernel(main_ref, rim_ref, place_ref, out_ref):
    added = spread_rim(rim_ref, place_ref)
    out_ref[...] = (main_ref[...].astype(F32) + added).astype(BF16)


def merge_kernel(weight_ref, own_ref, other_ref, out_ref):
    mixed = dot(weight_ref[0, 0, 0], own_ref[...]) + dot(weight_ref[0, 0, 1], other_ref[...])
    out_ref[...] = mixed.astype(BF16)


def slot_masks(ref, base, t, taps, bins, half):
    rows = ref[base : base + 4 * taps, :].astype(F32)
    beam = rows[t : t + 1]
    column = rows[taps + t : taps + t + 1]
    weight = rows[2 * taps + t : 2 * taps + t + 1] + rows[3 * taps + t : 3 * taps + t + 1]
    bin_ids = lax.broadcasted_iota(jnp.int32, (bins, ROW), 0).astype(F32)
    beam_ids = lax.broadcasted_iota(jnp.int32, (half, ROW), 0).astype(F32)
    pick_bin = (bin_ids == column).astype(F32).astype(BF16)
    return pick_bin, jnp.where(beam_ids == beam, weight, 0.0)


def mixed_kernel(weight_ref, begun_ref, own_rim_ref, other_rim_ref, place_ref, mixed_ref):
    rims = dot_nt(weight_ref[0, 0, 0], own_rim_ref[...])
    rims = rims + dot_nt(weight_ref[0, 0, 1], other_rim_ref[...])
    mixed_ref[...] = begun_ref[...] + dot(rims.astype(BF16), place_ref[...])


def ready_kernel(
    taps, weight_ref, own_ref, pack_ref, near_ref, pixel_ref,
    begun_ref, low_ref, high_ref, bin_ref, beam_ref,
):
    begun_ref[...] = dot(weight_ref[0, 0, 0], own_ref[...])
    half, bins = beam_ref.shape[1], bin_ref.shape[1]
    owners, slots = pixel_ref.shape[1:]
    for block, ref in enumerate((pack_ref, near_ref)):
        for t in range(taps):
            pick_bin, pick_beam = slot_masks(ref, half, t, taps, bins, half)
            bin_ref[block * taps + t] = pick_bin
            beam_ref[block * taps + t] = pick_beam
    pixel = jnp.concatenate([pixel_ref[0, b : b + 1, :] for b in range(owners)], 1)
    count = owners * slots
    low = lax.broadcasted_iota(jnp.int32, (LANES, count), 0) == (pixel & (LANES - 1))
    low_ref[...] = low.astype(F32).astype(BF16)
    tall = high_ref.shape[0]
    high = lax.broadcasted_iota(jnp.int32, (tall, count), 0) == pixel // LANES
    high_ref[...] = high.astype(F32)


def sample_kernel(
    taps, slots, chan_axis, weight_ref, mixed_ref, other_ref, pack_ref, near_ref, far_ref, *refs
):
    ready, out_ref = refs[:-1], refs[-1]
    size, bins = other_ref.shape
    half = size // 2
    mixed = mixed_ref[...] + dot(weight_ref[0, 0, 1], other_ref[...])
    polar = mixed.astype(BF16)
    chunks = (pack_ref.shape[0] - half) // (4 * taps)
    per_row = ROW // slots
    owners = per_row * chunks
    even = lax.axis_index(chan_axis) % 2 == 0
    far = jnp.concatenate([near_ref[:half, :], far_ref[:half, :]], 0)
    values = {}
    for block, (merge, ref) in enumerate(((weight_ref[0, 1, 0], pack_ref), (far, near_ref))):
        merged = dot(merge, polar).astype(BF16)
        for chunk in range(chunks):
            base = half + 4 * taps * chunk
            sums = [jnp.zeros((half, ROW), F32) for _ in range(2)]
            for t in range(taps):
                if ready:
                    pick_bin = ready[0][block * taps + t]
                    pick_beam = ready[1][block * taps + t]
                else:
                    pick_bin, pick_beam = slot_masks(ref, base, t, taps, bins, half)
                found = dot(merged, pick_bin)
                sums[0] = sums[0] + found[:half] * pick_beam
                sums[1] = sums[1] + found[half:] * pick_beam
            flat = [jnp.sum(value, axis=0, keepdims=True) for value in sums]
            if block == 1:
                flat = [jnp.where(even, flat[0], flat[1]), jnp.where(even, flat[1], flat[0])]
            values[chunk] = values.get(chunk, []) + flat
    for chunk in range(chunks):
        rows = [
            jnp.concatenate([v[:, k * slots : (k + 1) * slots] for v in values[chunk]], 1)
            for k in range(per_row)
        ]
        tile = jnp.concatenate(rows, 0)
        for copy in range(2):
            top = copy * owners + chunk * per_row
            out_ref[top : top + per_row, :] = tile


def scatter_kernel(slots, value_ref, low_ref, high_ref, out_ref):
    owners = value_ref.shape[0] // 2
    total = value_ref[:owners, :] + value_ref[owners:, :]
    flat = []
    for part in range(2):
        lane = part * slots
        own = total[:, lane : lane + slots]
        far = total[:, 2 * slots + lane : 2 * slots + lane + slots]
        far = jnp.concatenate([far[owners // 2 :], far[: owners // 2]], 0)
        both = own + far
        flat.append(jnp.concatenate([both[b : b + 1] for b in range(owners)], 1))
    high = high_ref[...]
    tall = high.shape[0]
    spread = jnp.concatenate([high * flat[part] for part in range(2)], 0)
    coarse = spread.astype(BF16)
    fine = (spread - coarse.astype(F32)).astype(BF16)
    low = low_ref[...]
    image = dot_nt(coarse, low) + dot_nt(fine, low)
    for part in range(2):
        for h in range(tall):
            row = part * tall + h
            out_ref[part : part + 1, h * LANES : (h + 1) * LANES] = image[row : row + 1, :]


def shape(dims, dtype):
    return jax.ShapeDtypeStruct(dims, dtype)


def call(kernel, out_shape, in_specs, out_specs, flops=0, nbytes=0, scratch=(), grid=None):
    extra = {} if grid is None else {"grid": grid}
    return pl.pallas_call(
        kernel,
        out_shape=out_shape,
        in_specs=in_specs,
        out_specs=out_specs,
        scratch_shapes=list(scratch),
        cost_estimate=pl.CostEstimate(flops=flops, bytes_accessed=nbytes, transcendentals=0),
        compiler_params=pltpu.CompilerParams(vmem_limit_bytes=24 * 2**20),
        **extra,
    )


def whole(array):
    return pl.BlockSpec(array.shape, lambda i: (0,) * array.ndim)


def swapped(value, axis, bit):
    return lax.ppermute(value, axis, [(i, i ^ 1 << bit) for i in range(lax.axis_size(axis))])


def neighbour_rims(rim):
    count = lax.axis_size("rng")
    if count == 2:
        return lax.ppermute(rim, "rng", [(0, 1), (1, 0)])
    after = lax.ppermute(rim, "rng", [(i + 1, i) for i in range(count - 1)])
    before = lax.ppermute(rim, "rng", [(i, i + 1) for i in range(count - 1)])
    return jnp.concatenate([after[:EDGE], before[EDGE:]], 0)


def local(raw, filt, steer, chan_w, merge_w, samp_index, samp_weight, counts, pixel_id):
    channels, _, pulses, bins = raw.shape
    size = steer.shape[1]
    levels = merge_w.shape[1]
    taps, owners, slots = samp_index.shape[1:]
    extra = 4 * taps * owners * slots // ROW
    blocks = lax.axis_size("rng")
    place = call(
        functools.partial(place_kernel, "rng", blocks),
        shape((2 * EDGE, bins), BF16),
        [],
        VMEM,
        flops=2**32,
        nbytes=2**24,
    )()
    pack = call(
        functools.partial(pack_kernel, bins.bit_length() - 1, "chan"),
        shape((size // 2 + extra, ROW), BF16),
        [VMEM] * 7,
        VMEM,
    )(merge_w, samp_index, samp_weight, counts, place, filt, chan_w)
    near = swapped(pack, "sub", levels - 1)
    bands, outer, mix = call(
        functools.partial(filter_kernel, bins),
        (
            shape((channels, 2, bins, bins), BF16),
            shape((channels, 2, 2 * EDGE, bins), BF16),
            shape((16 * channels, bins), F32),
        ),
        [VMEM] * 2,
        (VMEM,) * 3,
    )(filt, chan_w)
    main, rim = call(
        image_kernel,
        (shape((size, bins), BF16), shape((2 * EDGE, size), BF16)),
        [VMEM] * 5,
        (VMEM,) * 2,
        flops=2**30,
        nbytes=2**21,
    )(raw, steer, bands, outer, mix)
    polar, own_rim = main, neighbour_rims(rim)
    if levels == 2 and blocks == 2:
        groups = lax.axis_size("sub") * blocks
        other_rim = lax.ppermute(rim, ("sub", "rng"), [(i, i ^ 3) for i in range(groups)])
    else:
        polar = call(whole_kernel, shape((size, bins), BF16), [VMEM] * 3, VMEM)(
            main, own_rim, place
        )
        own_rim = other_rim = jnp.zeros((2 * EDGE, size), BF16)
    far = swapped(lax.optimization_barrier((polar, near))[1], "chan", 0)
    for level in range(levels - 2):
        other = swapped(polar, "sub", level)
        polar = call(
            merge_kernel,
            shape((size, bins), BF16),
            [
                pl.BlockSpec((1, 1, 2, size, size), lambda i, level=level: (0, level, 0, 0, 0)),
                whole(polar),
                whole(other),
            ],
            pl.BlockSpec((size, bins), lambda i: (0, 0)),
            grid=(1,),
        )(merge_w, polar, other)
    other = swapped(polar, "sub", levels - 2)
    chunks = owners * slots // ROW
    tall = PIX_OWN // LANES
    count = owners * slots
    sets = 2 * taps
    weights = merge_w[:, levels - 2 :]
    begun, low, high, *ready = call(
        functools.partial(ready_kernel, taps),
        (
            shape((size, bins), F32),
            shape((LANES, count), BF16),
            shape((tall, count), F32),
            shape((sets, bins, ROW), BF16),
            shape((sets, size // 2, ROW), F32),
        ),
        [VMEM] * 5,
        (VMEM,) * 5,
        flops=2**27,
        nbytes=2**19,
    )(weights, polar, pack, near, pixel_id)
    mixed = call(mixed_kernel, shape((size, bins), F32), [VMEM] * 5, VMEM, flops=2**30, nbytes=2**18)(
        weights, begun, own_rim, other_rim, place
    )
    if chunks > 1:
        ready = []
    outgoing = call(
        functools.partial(sample_kernel, taps, slots, "chan"),
        shape((2 * owners, 4 * slots), F32),
        [VMEM] * (6 + len(ready)),
        VMEM,
        flops=2**28,
        nbytes=2**20,
    )(weights, mixed, other, pack, near, far, *ready)
    values = lax.all_to_all(
        outgoing, ("chan", "sub", "rng"), split_axis=0, concat_axis=0, tiled=True
    )
    return call(
        functools.partial(scatter_kernel, slots), shape((2, PIX_OWN), F32), [VMEM] * 3, VMEM
    )(values, low, high)


def solution(mesh):
    placed = (
        P("chan", None, ("groups", "sub"), "rng"),
        P("chan", None, None),
        P("sub", None, None),
        P("chan", None),
        P("sub", None, None, None, None),
        P(("sub", "rng"), None, None, None),
        P(("sub", "rng"), None, None, None),
        P(("sub", "rng"), None),
        P(("sub", "rng"), None, None),
    )
    return jax.shard_map(
        local,
        mesh=mesh,
        in_specs=placed,
        out_specs=P(None, ("groups", "sub", "rng")),
        check_vma=False,
    )
```

```python
import functools

import jax
import jax.numpy as jnp
from jax import lax
from jax.experimental import pallas as pl
from jax.experimental.pallas import tpu as pltpu
from jax.sharding import PartitionSpec as P

PIX_OWN = 4096
LANES = 128
ROW = 256
EDGE = 8
F32 = jnp.float32
BF16 = jnp.bfloat16
VMEM = pl.BlockSpec(memory_space=pltpu.VMEM)
NT = (((1,), (1,)), ((), ()))


def dot(a, b):
    return jnp.dot(a, b, preferred_element_type=F32)


def dot_nt(a, b):
    return lax.dot_general(a, b, NT, preferred_element_type=F32)


def place_kernel(rng_axis, rng_size, place_ref):
    bins = place_ref.shape[1]
    block = lax.axis_index(rng_axis)
    row = lax.broadcasted_iota(jnp.int32, (2 * EDGE, bins), 0)
    column = lax.broadcasted_iota(jnp.int32, (2 * EDGE, bins), 1)
    after = jnp.where(block < rng_size - 1, bins - EDGE, 2 * bins)
    before = jnp.where(block > 0, -EDGE, 2 * bins)
    here = column == row + jnp.where(row < EDGE, after, before)
    place_ref[...] = here.astype(F32).astype(BF16)


def pack_kernel(
    shift, chan_axis, merge_ref, index_ref, weight_ref, counts_ref, _first, _filt, _mix, pack_ref
):
    half = merge_ref.shape[3] // 2
    last = merge_ref.shape[1] - 1
    core = lax.axis_index(chan_axis) % 2
    rows = pl.ds(pl.multiple_of(core * half, half), half)
    pack_ref[:half, :] = merge_ref[0, last, 1, rows, :]
    taps, owners, slots = index_ref.shape[1:]
    per_row = ROW // slots
    slot = lax.broadcasted_iota(jnp.int32, (taps, slots), 1)
    for first in range(0, owners, per_row):
        index = jnp.concatenate([index_ref[0, :, first + k, :] for k in range(per_row)], 1)
        weight = jnp.concatenate(
            [
                jnp.where(slot < counts_ref[:, first + k : first + k + 1], weight_ref[0, :, first + k, :], 0.0)
                for k in range(per_row)
            ],
            1,
        )
        coarse = weight.astype(BF16).astype(F32)
        beam = (index >> shift).astype(F32)
        column = (index & ((1 << shift) - 1)).astype(F32)
        lines = jnp.concatenate([beam, column, coarse, weight - coarse], 0).astype(BF16)
        base = half + 4 * taps * (first // per_row)
        pack_ref[base : base + 4 * taps, :] = lines


def filter_kernel(bins, filt_ref, chan_ref, band_ref, outer_ref, mix_ref):
    channels, parts, taps = filt_ref.shape
    rows = jnp.concatenate([filt_ref[c] for c in range(channels)], 0).astype(BF16)
    source = lax.broadcasted_iota(jnp.int32, (taps, LANES), 0)
    target = lax.broadcasted_iota(jnp.int32, (taps, LANES), 1)
    mirror = (source == ((EDGE - target) & (LANES - 1))).astype(F32).astype(BF16)
    bases = dot(rows, mirror)
    forward = dot(rows, (source == target).astype(F32).astype(BF16))
    row = lax.broadcasted_iota(jnp.int32, (LANES, LANES), 0)
    column = lax.broadcasted_iota(jnp.int32, (LANES, LANES), 1)
    far = column - row
    zero = jnp.zeros((LANES, LANES), BF16)
    count = bins // LANES
    low = lax.broadcasted_iota(jnp.int32, (EDGE, LANES), 1) < LANES // 2
    blank = jnp.zeros((EDGE, bins - LANES), F32)

    def turning(base, size, shift):
        wide = jnp.broadcast_to(base, (size, LANES))
        return pltpu.roll(wide, shift, 1, stride=1, stride_axis=0)

    for c in range(channels):
        for part in range(parts):
            line = slice(c * parts + part, c * parts + part + 1)
            ring = turning(bases[line], LANES, 0)
            blocks = {
                0: jnp.where((far < 64) & (far > -64), ring, 0.0).astype(BF16),
                1: jnp.where(far >= 64, ring, 0.0).astype(BF16),
                -1: jnp.where(far <= -64, ring, 0.0).astype(BF16),
            }
            for i in range(count):
                for o in range(count):
                    band_ref[
                        c, part, i * LANES : (i + 1) * LANES, o * LANES : (o + 1) * LANES
                    ] = blocks.get(i - o, zero)
            lower = jnp.where(low, turning(forward[line], EDGE, LANES - 2 * EDGE), 0.0)
            upper = jnp.where(low, 0.0, turning(forward[line], EDGE, LANES - EDGE))
            outer = jnp.concatenate(
                [jnp.concatenate([lower, blank], 1), jnp.concatenate([blank, upper], 1)], 0
            )
            outer_ref[c, part] = outer.astype(BF16)
            mix_ref[8 * (2 * c + part) : 8 * (2 * c + part + 1), :] = jnp.broadcast_to(
                chan_ref[c : c + 1, part : part + 1], (8, bins)
            )


def turned(value, mix_ref, channel):
    half = value.shape[0] // 2
    re, im = value[:half], value[half:]
    wr = mix_ref[16 * channel : 16 * channel + 1, :]
    wi = mix_ref[16 * channel + 8 : 16 * channel + 9, :]
    return jnp.concatenate([wr * re - wi * im, wr * im + wi * re], 0)


def image_kernel(raw_ref, steer_ref, band_ref, outer_ref, mix_ref, out_ref, rim_ref):
    channels, _, pulses, _ = raw_ref.shape
    s_re, s_im = steer_ref[0, :, :pulses], steer_ref[0, :, pulses:]
    half = steer_ref.shape[1] // 2
    total = jnp.zeros(out_ref.shape, F32)
    rim = jnp.zeros(rim_ref.shape, F32)
    crossed = jnp.concatenate([s_im, -s_re], 1)
    for c in range(channels):
        echoes = raw_ref[c].reshape(2 * pulses, raw_ref.shape[3])
        direct = dot(steer_ref[0], echoes).astype(BF16)
        cross = dot(crossed, echoes).astype(BF16)
        image = dot(direct, band_ref[c, 0]) + dot(cross, band_ref[c, 1])
        total = total + turned(image, mix_ref, c)
        side = dot_nt(outer_ref[c, 0], direct) + dot_nt(outer_ref[c, 1], cross)
        re, im = side[:, :half], side[:, half:]
        wr = mix_ref[16 * c : 16 * c + 1, :half]
        wi = mix_ref[16 * c + 8 : 16 * c + 9, :half]
        rim = rim + jnp.concatenate([wr * re - wi * im, wr * im + wi * re], 1)
    out_ref[...] = total.astype(BF16)
    rim_ref[...] = rim.astype(BF16)


def spread_rim(rim_ref, place_ref):
    return lax.dot_general(
        rim_ref[...], place_ref[...], (((0,), (0,)), ((), ())), preferred_element_type=F32
    )


def whole_kernel(main_ref, rim_ref, place_ref, out_ref):
    added = spread_rim(rim_ref, place_ref)
    out_ref[...] = (main_ref[...].astype(F32) + added).astype(BF16)


def merge_kernel(weight_ref, own_ref, other_ref, out_ref):
    mixed = dot(weight_ref[0, 0, 0], own_ref[...]) + dot(weight_ref[0, 0, 1], other_ref[...])
    out_ref[...] = mixed.astype(BF16)


def slot_masks(ref, base, t, taps, bins, half):
    rows = ref[base : base + 4 * taps, :].astype(F32)
    beam = rows[t : t + 1]
    column = rows[taps + t : taps + t + 1]
    weight = rows[2 * taps + t : 2 * taps + t + 1] + rows[3 * taps + t : 3 * taps + t + 1]
    bin_ids = lax.broadcasted_iota(jnp.int32, (bins, ROW), 0).astype(F32)
    beam_ids = lax.broadcasted_iota(jnp.int32, (half, ROW), 0).astype(F32)
    pick_bin = (bin_ids == column).astype(F32).astype(BF16)
    return pick_bin, jnp.where(beam_ids == beam, weight, 0.0)


def mixed_kernel(weight_ref, begun_ref, own_rim_ref, other_rim_ref, place_ref, mixed_ref):
    rims = dot_nt(weight_ref[0, 0, 0], own_rim_ref[...])
    rims = rims + dot_nt(weight_ref[0, 0, 1], other_rim_ref[...])
    mixed_ref[...] = begun_ref[...] + dot(rims.astype(BF16), place_ref[...])


def ready_kernel(
    taps, weight_ref, own_ref, pack_ref, near_ref, pixel_ref,
    begun_ref, low_ref, high_ref, bin_ref, beam_ref,
):
    begun_ref[...] = dot(weight_ref[0, 0, 0], own_ref[...])
    half, bins = beam_ref.shape[1], bin_ref.shape[1]
    owners, slots = pixel_ref.shape[1:]
    for block, ref in enumerate((pack_ref, near_ref)):
        for t in range(taps):
            pick_bin, pick_beam = slot_masks(ref, half, t, taps, bins, half)
            bin_ref[block * taps + t] = pick_bin
            beam_ref[block * taps + t] = pick_beam
    pixel = jnp.concatenate([pixel_ref[0, b : b + 1, :] for b in range(owners)], 1)
    count = owners * slots
    low = lax.broadcasted_iota(jnp.int32, (LANES, count), 0) == (pixel & (LANES - 1))
    low_ref[...] = low.astype(F32).astype(BF16)
    tall = high_ref.shape[0]
    high = lax.broadcasted_iota(jnp.int32, (tall, count), 0) == pixel // LANES
    high_ref[...] = high.astype(F32)


def sample_kernel(
    taps, slots, chan_axis, weight_ref, mixed_ref, other_ref, pack_ref, near_ref, far_ref, *refs
):
    ready, out_ref = refs[:-1], refs[-1]
    size, bins = other_ref.shape
    half = size // 2
    mixed = mixed_ref[...] + dot(weight_ref[0, 0, 1], other_ref[...])
    polar = mixed.astype(BF16)
    chunks = (pack_ref.shape[0] - half) // (4 * taps)
    per_row = ROW // slots
    owners = per_row * chunks
    even = lax.axis_index(chan_axis) % 2 == 0
    far = jnp.concatenate([near_ref[:half, :], far_ref[:half, :]], 0)
    values = {}
    for block, (merge, ref) in enumerate(((weight_ref[0, 1, 0], pack_ref), (far, near_ref))):
        merged = dot(merge, polar).astype(BF16)
        for chunk in range(chunks):
            base = half + 4 * taps * chunk
            sums = [jnp.zeros((half, ROW), F32) for _ in range(2)]
            for t in range(taps):
                if ready:
                    pick_bin = ready[0][block * taps + t]
                    pick_beam = ready[1][block * taps + t]
                else:
                    pick_bin, pick_beam = slot_masks(ref, base, t, taps, bins, half)
                found = dot(merged, pick_bin)
                sums[0] = sums[0] + found[:half] * pick_beam
                sums[1] = sums[1] + found[half:] * pick_beam
            flat = [jnp.sum(value, axis=0, keepdims=True) for value in sums]
            if block == 1:
                flat = [jnp.where(even, flat[0], flat[1]), jnp.where(even, flat[1], flat[0])]
            values[chunk] = values.get(chunk, []) + flat
    for chunk in range(chunks):
        rows = [
            jnp.concatenate([v[:, k * slots : (k + 1) * slots] for v in values[chunk]], 1)
            for k in range(per_row)
        ]
        tile = jnp.concatenate(rows, 0)
        for copy in range(2):
            top = copy * owners + chunk * per_row
            out_ref[top : top + per_row, :] = tile


def scatter_kernel(slots, value_ref, low_ref, high_ref, out_ref):
    owners = value_ref.shape[0] // 2
    total = value_ref[:owners, :] + value_ref[owners:, :]
    flat = []
    for part in range(2):
        lane = part * slots
        own = total[:, lane : lane + slots]
        far = total[:, 2 * slots + lane : 2 * slots + lane + slots]
        far = jnp.concatenate([far[owners // 2 :], far[: owners // 2]], 0)
        both = own + far
        flat.append(jnp.concatenate([both[b : b + 1] for b in range(owners)], 1))
    high = high_ref[...]
    tall = high.shape[0]
    spread = jnp.concatenate([high * flat[part] for part in range(2)], 0)
    coarse = spread.astype(BF16)
    fine = (spread - coarse.astype(F32)).astype(BF16)
    low = low_ref[...]
    image = dot_nt(coarse, low) + dot_nt(fine, low)
    for part in range(2):
        for h in range(tall):
            row = part * tall + h
            out_ref[part : part + 1, h * LANES : (h + 1) * LANES] = image[row : row + 1, :]


def shape(dims, dtype):
    return jax.ShapeDtypeStruct(dims, dtype)


def call(kernel, out_shape, in_specs, out_specs, flops=0, nbytes=0, scratch=(), grid=None):
    extra = {} if grid is None else {"grid": grid}
    return pl.pallas_call(
        kernel,
        out_shape=out_shape,
        in_specs=in_specs,
        out_specs=out_specs,
        scratch_shapes=list(scratch),
        cost_estimate=pl.CostEstimate(flops=flops, bytes_accessed=nbytes, transcendentals=0),
        compiler_params=pltpu.CompilerParams(vmem_limit_bytes=24 * 2**20),
        **extra,
    )


def whole(array):
    return pl.BlockSpec(array.shape, lambda i: (0,) * array.ndim)


def swapped(value, axis, bit):
    return lax.ppermute(value, axis, [(i, i ^ 1 << bit) for i in range(lax.axis_size(axis))])


def neighbour_rims(rim):
    count = lax.axis_size("rng")
    if count == 2:
        return lax.ppermute(rim, "rng", [(0, 1), (1, 0)])
    after = lax.ppermute(rim, "rng", [(i + 1, i) for i in range(count - 1)])
    before = lax.ppermute(rim, "rng", [(i, i + 1) for i in range(count - 1)])
    return jnp.concatenate([after[:EDGE], before[EDGE:]], 0)


def local(raw, filt, steer, chan_w, merge_w, samp_index, samp_weight, counts, pixel_id):
    channels, _, pulses, bins = raw.shape
    size = steer.shape[1]
    levels = merge_w.shape[1]
    taps, owners, slots = samp_index.shape[1:]
    extra = 4 * taps * owners * slots // ROW
    blocks = lax.axis_size("rng")
    place = call(
        functools.partial(place_kernel, "rng", blocks),
        shape((2 * EDGE, bins), BF16),
        [],
        VMEM,
        flops=2**32,
        nbytes=2**24,
    )()
    pack = call(
        functools.partial(pack_kernel, bins.bit_length() - 1, "chan"),
        shape((size // 2 + extra, ROW), BF16),
        [VMEM] * 7,
        VMEM,
    )(merge_w, samp_index, samp_weight, counts, place, filt, chan_w)
    near = swapped(pack, "sub", levels - 1)
    bands, outer, mix = call(
        functools.partial(filter_kernel, bins),
        (
            shape((channels, 2, bins, bins), BF16),
            shape((channels, 2, 2 * EDGE, bins), BF16),
            shape((16 * channels, bins), F32),
        ),
        [VMEM] * 2,
        (VMEM,) * 3,
    )(filt, chan_w)
    main, rim = call(
        image_kernel,
        (shape((size, bins), BF16), shape((2 * EDGE, size), BF16)),
        [VMEM] * 5,
        (VMEM,) * 2,
        flops=2**30,
        nbytes=2**21,
    )(raw, steer, bands, outer, mix)
    polar, own_rim = main, neighbour_rims(rim)
    if levels == 2 and blocks == 2:
        groups = lax.axis_size("sub") * blocks
        other_rim = lax.ppermute(rim, ("sub", "rng"), [(i, i ^ 3) for i in range(groups)])
    else:
        polar = call(whole_kernel, shape((size, bins), BF16), [VMEM] * 3, VMEM)(
            main, own_rim, place
        )
        own_rim = other_rim = jnp.zeros((2 * EDGE, size), BF16)
    far = swapped(lax.optimization_barrier((polar, near))[1], "chan", 0)
    for level in range(levels - 2):
        other = swapped(polar, "sub", level)
        polar = call(
            merge_kernel,
            shape((size, bins), BF16),
            [
                pl.BlockSpec((1, 1, 2, size, size), lambda i, level=level: (0, level, 0, 0, 0)),
                whole(polar),
                whole(other),
            ],
            pl.BlockSpec((size, bins), lambda i: (0, 0)),
            grid=(1,),
        )(merge_w, polar, other)
    other = swapped(polar, "sub", levels - 2)
    chunks = owners * slots // ROW
    tall = PIX_OWN // LANES
    count = owners * slots
    sets = 2 * taps
    weights = merge_w[:, levels - 2 :]
    begun, low, high, *ready = call(
        functools.partial(ready_kernel, taps),
        (
            shape((size, bins), F32),
            shape((LANES, count), BF16),
            shape((tall, count), F32),
            shape((sets, bins, ROW), BF16),
            shape((sets, size // 2, ROW), F32),
        ),
        [VMEM] * 5,
        (VMEM,) * 5,
        flops=2**27,
        nbytes=2**19,
    )(weights, polar, pack, near, pixel_id)
    mixed = call(mixed_kernel, shape((size, bins), F32), [VMEM] * 5, VMEM, flops=2**30, nbytes=2**18)(
        weights, begun, own_rim, other_rim, place
    )
    if chunks > 1:
        ready = []
    outgoing = call(
        functools.partial(sample_kernel, taps, slots, "chan"),
        shape((2 * owners, 4 * slots), F32),
        [VMEM] * (6 + len(ready)),
        VMEM,
        flops=2**28,
        nbytes=2**20,
    )(weights, mixed, other, pack, near, far, *ready)
    values = lax.all_to_all(
        outgoing, ("chan", "sub", "rng"), split_axis=0, concat_axis=0, tiled=True
    )
    return call(
        functools.partial(scatter_kernel, slots), shape((2, PIX_OWN), F32), [VMEM] * 3, VMEM
    )(values, low, high)


def solution(mesh):
    placed = (
        P("chan", None, ("groups", "sub"), "rng"),
        P("chan", None, None),
        P("sub", None, None),
        P("chan", None),
        P("sub", None, None, None, None),
        P(("sub", "rng"), None, None, None),
        P(("sub", "rng"), None, None, None),
        P(("sub", "rng"), None),
        P(("sub", "rng"), None, None),
    )
    return jax.shard_map(
        local,
        mesh=mesh,
        in_specs=placed,
        out_specs=P(None, ("groups", "sub", "rng")),
        check_vma=False,
    )
```
